128 devices in a mesh: lon: 32 (over y_hi, z, x), lat: 4 (over y_lo, core).
Axes of the slice: x: 4, y: 4 (y_hi: 2, y_lo: 2; y = y_hi * 2 + y_lo), z: 4, core: 2. Of those that a mesh axis runs over, the one named last changes fastest.
Arguments:
- fine_field: bfloat16 [2, 96, 768, 512], P(None, 'lat', 'lon'), may hold values from -6 to 6
- head_scale: float32 [16], replicated, may hold values from 2 to 16
- qkv_weight: bfloat16 [512, 1536], replicated, may hold values from -0.25 to 0.25
- out_weight: bfloat16 [512, 512], replicated, may hold values from -0.25 to 0.25
- merge_weight: bfloat16 [2048, 1024], replicated, may hold values from -0.125 to 0.125
- up_weight: bfloat16 [1024, 4096], P('lon', 'lat'), may hold values from -0.1875 to 0.1875
- down_weight: bfloat16 [4096, 1024], P('lat', 'lon'), may hold values from -0.09375 to 0.09375
- cotangent: bfloat16 [2, 48, 384, 1024], P(None, 'lat', 'lon'), may hold values from -6 to 6
Outputs:
- skip_field: bfloat16 [2, 96, 768, 512], P(None, 'lat', 'lon')
- coarse_out: bfloat16 [2, 48, 384, 1024], P(None, 'lat', 'lon')
- up_grad: float32 [1024, 4096], P('lon', 'lat')
- down_grad: float32 [4096, 1024], P('lat', 'lon')
- skip_grad: float32 [2, 96, 768, 512], P(None, 'lat', 'lon')
The draws below stay inside these ranges and needn't reach their ends.
All inputs are finite; a program needn't handle non-finite values.
Results may differ from the reference program's by a relative error of at most 0.03.
Values may be sent and summed in bfloat16 or wider, within the bound.
No kernel may reach another device: no remote copies, remote signals or barrier semaphores. Data moves between devices by JAX's collectives and lax.ppermute only.
A program may use at most 192 MiB of HBM per device.

```python
import math
import jax
import jax.numpy as jnp
from jax import lax

C = 512
HEADS = 16
D2 = 1024
FF2 = 4096
LEV = 2
WH = 6
WW = 12
H = 96
W = 768
N_LAT = 4


def level_of(stream_key, extent, shards, least, top_value):
    def one(position, parts):
        draws = jax.random.uniform(jax.random.fold_in(jax.random.fold_in(stream_key, 6), position), (parts,), jnp.float32, least / len(shards), top_value / len(shards))
        return jnp.repeat(jnp.exp(draws), extent[position] // parts).reshape((-1,) + (1,) * (len(extent) - position - 1))

    loudness = one(*shards[0])
    for cut in shards[1:]:
        loudness = loudness * one(*cut)
    return loudness


def bell_draw(rng, extent, spread, reach, shards=(), kind=jnp.bfloat16):
    values = spread * jax.random.normal(rng, extent, jnp.float32)
    if shards:
        values = values * level_of(rng, extent, shards, -0.22, 0.18)
    return jnp.clip(values, -reach, reach).astype(kind)


def setup_inputs(seed: int = 0) -> dict:
    streams_of = jax.random.split(jax.random.key(seed), 9)
    fine_field = bell_draw(streams_of[0], (LEV, H, W, C), 1.0, 6.0, ((1, 4), (2, 32)))
    head_scale = jnp.clip(jnp.exp(jax.random.uniform(streams_of[1], (HEADS,), jnp.float32, math.log(2.0), math.log(16.0))), 2.0, 16.0)
    qkv_weight = bell_draw(streams_of[2], (C, 3 * C), C ** -0.5, 0.25)
    out_weight = bell_draw(streams_of[3], (C, C), C ** -0.5, 0.25)
    merge_weight = bell_draw(streams_of[4], (4 * C, D2), (4 * C) ** -0.5, 0.125)
    up_weight = bell_draw(streams_of[5], (D2, FF2), D2 ** -0.5, 0.1875, ((0, 32), (1, 4)))
    down_weight = bell_draw(streams_of[6], (FF2, D2), FF2 ** -0.5, 0.09375, ((0, 4), (1, 32)))
    cotangent = bell_draw(streams_of[7], (LEV, H // 2, W // 2, D2), 1.0, 6.0, ((1, 4), (2, 32)))
    return dict(fine_field=fine_field, head_scale=head_scale, qkv_weight=qkv_weight, out_weight=out_weight, merge_weight=merge_weight, up_weight=up_weight, down_weight=down_weight, cotangent=cotangent)


def layer_norm(inputs):
    average = lax.optimization_barrier(jnp.mean(inputs, -1, keepdims=True))
    centred = inputs - average
    return centred * lax.rsqrt(lax.optimization_barrier(jnp.mean(centred * centred, -1, keepdims=True)) + 1e-05)

def gelu_exact(inputs):
    return jax.nn.gelu(inputs, approximate=False)

def merge_tokens(fine):
    levels, lat_rows, lon_cols, channels = fine.shape
    pieces = fine.reshape(levels, lat_rows // 2, 2, lon_cols // 2, 2, channels)
    return pieces.transpose(0, 1, 3, 4, 2, 5).reshape(levels, lat_rows // 2, lon_cols // 2, 4 * channels)

def split_tokens(coarse):
    levels, lat_rows, lon_cols, merged = coarse.shape
    pieces = coarse.reshape(levels, lat_rows, lon_cols, 2, 2, merged // 4)
    return pieces.transpose(0, 1, 4, 2, 3, 5).reshape(levels, 2 * lat_rows, 2 * lon_cols, merged // 4)

def window_attention(qkv_win, group, head_scale):
    windows_count, window_tokens, triple_width = qkv_win.shape
    channels = triple_width // 3
    head_count = head_scale.shape[0]
    sections = qkv_win.reshape(windows_count, window_tokens, 3, head_count, channels // head_count)
    queries = sections[:, :, 0].astype(jnp.float32)
    key_vectors = sections[:, :, 1].astype(jnp.float32)
    value_vectors = sections[:, :, 2].astype(jnp.float32)
    queries = queries * lax.rsqrt(lax.optimization_barrier(jnp.sum(queries * queries, -1, keepdims=True)) + 1e-06)
    key_vectors = key_vectors * lax.rsqrt(lax.optimization_barrier(jnp.sum(key_vectors * key_vectors, -1, keepdims=True)) + 1e-06)
    scores = jnp.einsum('nqhd,nkhd->nhqk', queries, key_vectors, precision=lax.Precision.HIGHEST)
    scores = scores * head_scale[None, :, None, None]
    same_group = (group[:, :, None] == group[:, None, :])[:, None]
    expsum = jnp.where(same_group, jnp.exp(scores), jnp.zeros_like(scores))
    attn_weights = (expsum / lax.optimization_barrier(jnp.sum(expsum, -1, keepdims=True))).astype(jnp.bfloat16)
    attended = jnp.einsum('nhqk,nkhd->nqhd', attn_weights.astype(jnp.float32), value_vectors)
    return attended.reshape(windows_count, window_tokens, channels).astype(jnp.bfloat16)

def reference(fine_field, head_scale, qkv_weight, out_weight, merge_weight, up_weight, down_weight, cotangent):
    levels, lat_rows, lon_cols, channels = fine_field.shape
    fine32 = fine_field.astype(jnp.float32)
    normed_fine = layer_norm(fine32).astype(jnp.bfloat16)
    qkv = jnp.dot(normed_fine.reshape(-1, channels), qkv_weight, preferred_element_type=jnp.float32).astype(jnp.bfloat16)
    qkv = jnp.roll(qkv.reshape(levels, lat_rows, lon_cols, 3 * channels), (-(WH // 2), -(WW // 2)), axis=(1, 2))
    band_count = lat_rows // WH
    column_windows = lon_cols // WW
    windows = qkv.reshape(levels, band_count, WH, column_windows, WW, 3 * channels).transpose(1, 3, 0, 2, 4, 5)
    windows = windows.reshape(band_count, column_windows, levels * WH * WW, 3 * channels)
    anchor_rows = (jnp.arange(lat_rows, dtype=jnp.int32) + WH // 2) % lat_rows
    row_group = (anchor_rows < WH // 2).astype(jnp.int32).reshape(band_count, 1, 1, WH, 1)
    token_group = jnp.broadcast_to(row_group, (band_count, column_windows, levels, WH, WW))
    token_group = token_group.reshape(band_count, column_windows, levels * WH * WW)
    attended = lax.map(lambda inputs_pair: window_attention(inputs_pair[0], inputs_pair[1], head_scale), (windows, token_group))
    attended = attended.reshape(band_count, column_windows, levels, WH, WW, channels).transpose(2, 0, 3, 1, 4, 5)
    attended = jnp.roll(attended.reshape(levels, lat_rows, lon_cols, channels), (WH // 2, WW // 2), axis=(1, 2))
    projected = jnp.dot(attended.reshape(-1, channels), out_weight, preferred_element_type=jnp.float32)
    skip_field = (fine32 + projected.reshape(levels, lat_rows, lon_cols, channels)).astype(jnp.bfloat16)
    concat = merge_tokens(skip_field.astype(jnp.float32))
    concat_flat = concat.reshape(-1, 4 * channels)
    concat_norm = layer_norm(concat_flat).astype(jnp.bfloat16)
    coarse_field = jnp.dot(concat_norm, merge_weight, preferred_element_type=jnp.float32).astype(jnp.bfloat16)
    coarse32 = coarse_field.astype(jnp.float32)
    normed_coarse = layer_norm(coarse32).astype(jnp.bfloat16)
    grad_flat = cotangent.reshape(-1, D2)
    ff_block = FF2 // N_LAT
    summed = jnp.zeros(coarse32.shape, jnp.float32)
    normed_grad = jnp.zeros(coarse32.shape, jnp.float32)
    up_grads = []
    down_grads = []
    for part_index in range(N_LAT):
        up_block = up_weight[:, part_index * ff_block:(part_index + 1) * ff_block]
        down_block = down_weight[part_index * ff_block:(part_index + 1) * ff_block]
        pre_act = jnp.dot(normed_coarse, up_block, preferred_element_type=jnp.float32)
        hidden = gelu_exact(pre_act).astype(jnp.bfloat16)
        partial_out = jnp.dot(hidden, down_block, preferred_element_type=jnp.float32).astype(jnp.bfloat16)
        summed = summed + lax.optimization_barrier(partial_out).astype(jnp.float32)
        hidden_grad = jnp.dot(grad_flat, down_block.T, preferred_element_type=jnp.float32)
        gelu_back = jax.vjp(gelu_exact, pre_act)[1]
        pre_grad = gelu_back(hidden_grad)[0].astype(jnp.bfloat16)
        down_grads.append(jnp.dot(hidden.T, grad_flat, preferred_element_type=jnp.float32))
        up_grads.append(jnp.dot(normed_coarse.T, pre_grad, preferred_element_type=jnp.float32))
        back_part = jnp.dot(pre_grad, up_block.T, preferred_element_type=jnp.float32).astype(jnp.bfloat16)
        normed_grad = normed_grad + lax.optimization_barrier(back_part).astype(jnp.float32)
    coarse_out = (coarse32 + summed).astype(jnp.bfloat16).reshape(levels, lat_rows // 2, lon_cols // 2, D2)
    up_grad = jnp.concatenate(up_grads, 1)
    down_grad = jnp.concatenate(down_grads, 0)
    norm_back = jax.vjp(layer_norm, coarse32)[1]
    coarse_grad = (grad_flat.astype(jnp.float32) + norm_back(normed_grad)[0]).astype(jnp.bfloat16)
    cat_grad = jnp.dot(coarse_grad, merge_weight.T, preferred_element_type=jnp.float32)
    cat_back = jax.vjp(layer_norm, concat_flat)[1]
    concat_grad = cat_back(cat_grad)[0].reshape(concat.shape)
    skip_grad = split_tokens(concat_grad)
    return (skip_field, coarse_out, up_grad, down_grad, skip_grad)
```

```python
import functools
import math

import jax
import jax.numpy as jnp
import numpy as np
from jax import lax
from jax.experimental import pallas as pl
from jax.experimental.pallas import tpu as pltpu
from jax.sharding import PartitionSpec as P

WH = 6
WW = 12
HEAD = 32
LANES = 128
GROUP = 4
F32 = jnp.float32
BF16 = jnp.bfloat16
VMEM_BYTES = 56 * 1024 * 1024

WHOLE = pl.BlockSpec(memory_space=pltpu.VMEM)
SCALARS = pl.BlockSpec(memory_space=pltpu.SMEM)
LEFT_OUT = pl.BlockSpec(memory_space=pl.ANY)


def run_kernel(body, name, specs, outs, scratch, flops, moved, *operands):
    return pl.pallas_call(
        body,
        name=name,
        in_specs=specs,
        out_specs=[WHOLE] * len(outs),
        out_shape=outs,
        scratch_shapes=scratch,
        compiler_params=pltpu.CompilerParams(vmem_limit_bytes=VMEM_BYTES),
        cost_estimate=pl.CostEstimate(flops=flops, bytes_accessed=moved, transcendentals=0),
    )(*operands)


def shaped(shape, kind):
    return jax.ShapeDtypeStruct(shape, kind)


def dot_nn(left, right):
    return lax.dot_general(left, right, (((1,), (0,)), ((), ())), preferred_element_type=F32)


def dot_nt(left, right):
    return lax.dot_general(left, right, (((1,), (1,)), ((), ())), preferred_element_type=F32)


def dot_tn(left, right):
    return lax.dot_general(left, right, (((0,), (0,)), ((), ())), preferred_element_type=F32)


def centre_scale(rows):
    centred = rows - jnp.mean(rows, -1, keepdims=True)
    inverse = lax.rsqrt(jnp.mean(centred * centred, -1, keepdims=True) + 1e-05)
    return centred * inverse, inverse


def lon_dims(count):
    return (count // 16, 4, 4) if count % 16 == 0 else (count, 1, 1)


def lon_strides(dims):
    return (dims[1] * dims[2], dims[2], 1)


def lon_pairs(count, digit, step):
    dims = lon_dims(count)
    stride = lon_strides(dims)[digit]
    pairs = []
    for i in range(count):
        d = (i // stride) % dims[digit]
        pairs.append((i, i + ((d + step) % dims[digit] - d) * stride))
    return pairs


def lat_swap(array, bit):
    count = lax.axis_size("lat")
    return lax.ppermute(array, "lat", [(i, i ^ bit) for i in range(count)])


def gather_lon(piece, order):
    count = lax.axis_size("lon")
    dims = lon_dims(count)
    stack = piece[None]
    for at, digit in enumerate(order):
        parts = [stack] + [
            lax.ppermute(stack, "lon", lon_pairs(count, digit, -k)) for k in range(1, dims[digit])
        ]
        stack = parts if at == 2 else jnp.concatenate(parts, 0)
    return stack


def reduce_lon(blocks, order):
    count = lax.axis_size("lon")
    dims = lon_dims(count)
    for at, digit in enumerate(order):
        n = dims[digit]
        share = blocks.shape[0] // n
        total = blocks[:share].astype(F32)
        for k in range(1, n):
            total = total + lax.ppermute(
                blocks[k * share : (k + 1) * share], "lon", lon_pairs(count, digit, k)
            ).astype(F32)
        blocks = total if at == 2 else total.astype(BF16)
    return blocks[0]


def front_body(
    half_lat, flag_ref, x_ref, top_ref, bot_ref, left_ref, right_ref, scale_ref, qkv_w, out_w,
    merge_hbm, mask_ref, ones_ref, lane_ref, sums_ref,
    skip_ref, cat_ref, coarse_ref, normed_ref,
    ext, xw, qkv, att, cat, catn, spread, merge_w, sem,
):
    levels, rows, cols, width = x_ref.shape
    fetch = pltpu.make_async_copy(merge_hbm, merge_w, sem)
    fetch.start()
    lead = 8
    half_lon = left_ref.shape[2]
    tokens = levels * WH * WW
    wins = (cols + 2 * half_lon) // WW

    def fill(row, carry):
        for l in range(levels):
            ext[l, half_lat + row, lead : lead + cols, :] = x_ref[l, row].astype(F32)
        return carry

    lax.fori_loop(0, rows, fill, 0)
    for l in range(levels):
        for r in range(half_lat):
            ext[l, r, lead : lead + cols, :] = top_ref[l, r].astype(F32)
            ext[l, half_lat + rows + r, lead : lead + cols, :] = bot_ref[l, r].astype(F32)

    def fill_sides(row, carry):
        for l in range(levels):
            ext[l, row, lead - half_lon : lead, :] = left_ref[l, row].astype(F32)
            ext[l, row, lead + cols : lead + cols + half_lon, :] = right_ref[l, row].astype(F32)
        return carry

    lax.fori_loop(0, rows + 2 * half_lat, fill_sides, 0)

    chunk = 256
    sections = width // chunk
    groups = width // (GROUP * HEAD)
    lanes = GROUP * HEAD

    def places():
        for c in range(wins):
            for l in range(levels):
                for r in range(WH):
                    yield c, l, r

    def band(b, carry):
        for c, l, r in places():
            at = c * tokens + (l * WH + r) * WW
            start = lead - half_lon + c * WW
            xw[at : at + WW, :] = ext[l, b * WH + r, start : start + WW, :]
        normed = centre_scale(xw[...])[0].astype(BF16)
        for j in range(3 * sections):
            y = dot_nn(normed, qkv_w[:, j * chunk : (j + 1) * chunk])
            if j < 2 * sections:
                square = y * y
                high = square.astype(BF16)
                low = (square - high.astype(F32)).astype(BF16)
                total = dot_nn(high, ones_ref[...]) + dot_nn(low, ones_ref[...])
                y = y * lax.rsqrt(total + 1e-06)
                if j < sections:
                    y = y * scale_ref[:, j * chunk : (j + 1) * chunk]
            qkv[:, j * chunk : (j + 1) * chunk] = y.astype(BF16)
        allowed = mask_ref[flag_ref[b]]
        for c in range(wins):
            rows_at = slice(c * tokens, (c + 1) * tokens)
            for g in range(groups):
                q = qkv[rows_at, g * lanes : (g + 1) * lanes]
                k = qkv[rows_at, width + g * lanes : width + (g + 1) * lanes]
                v = qkv[rows_at, 2 * width + g * lanes : 2 * width + (g + 1) * lanes]
                k4 = jnp.concatenate([k * lane_ref[h : h + 1, :] for h in range(GROUP)], 0)
                v4 = jnp.concatenate([v * lane_ref[h : h + 1, :] for h in range(GROUP)], 0)
                weight = jnp.exp2(dot_nt(q, k4)).astype(BF16) * allowed
                both = dot_nn(weight, jnp.concatenate([v4, sums_ref[...]], 1))
                att[rows_at, g * lanes : (g + 1) * lanes] = (
                    both[:, :lanes] / both[:, lanes:]
                ).astype(BF16)
        skip = xw[...] + dot_nn(att[...], out_w[...])
        xw[...] = skip.astype(BF16).astype(F32)
        for c, l, r in places():
            at = c * tokens + (l * WH + r) * WW
            start = lead - half_lon + c * WW
            ext[l, b * WH + r, start : start + WW, :] = xw[at : at + WW, :]
        return carry

    lax.fori_loop(0, (rows + 2 * half_lat) // WH, band, 0)

    def store_skip(row, carry):
        for l in range(levels):
            line = ext[l, half_lat + row, lead : lead + cols, :]
            skip_ref[l, row] = line.astype(BF16)
            for q in range(width // LANES):
                spread[l, row, q] = line[:, q * LANES : (q + 1) * LANES]
        return carry

    lax.fori_loop(0, rows, store_skip, 0)
    half = cols // 2
    for l in range(levels):
        for i in range(rows // 2):
            at = (l * (rows // 2) + i) * half
            for a in range(2):
                for b in range(2):
                    for q in range(width // LANES):
                        to = (a + 2 * b) * width + q * LANES
                        cat[at : at + half, to : to + LANES] = spread[
                            l, 2 * i + a, q, pl.ds(b, half, 2), :
                        ]
    total = cat.shape[0]
    step = 96
    for s in range(0, total, step):
        piece = cat[s : s + step, :]
        cat_ref[s : s + step, :] = piece.astype(BF16)
        catn[s : s + step, :] = centre_scale(piece)[0].astype(BF16)
    fetch.wait()
    coarse = dot_nn(catn[...], merge_w[...]).astype(BF16)
    coarse_ref[...] = coarse
    normed_ref[...] = centre_scale(coarse.astype(F32))[0].astype(BF16)


def front(fine, top, bot, left, right, head_scale, qkv_weight, out_weight, merge_weight):
    levels, rows, cols, width = fine.shape
    half_lat = WH // 2
    tokens = levels * WH * WW
    ext_rows = rows + 2 * half_lat
    bands = ext_rows // WH
    wins = (cols + WW) // WW
    heads = head_scale.shape[0]
    coarse_width = merge_weight.shape[1]
    coarse_tokens = levels * rows * cols // 4
    lat_place = lax.axis_index("lat")
    lat_last = lax.axis_size("lat") - 1
    band_ids = jnp.arange(bands)
    flags = (
        ((band_ids == 0) & (lat_place == 0)) | ((band_ids == bands - 1) & (lat_place == lat_last))
    ).astype(jnp.int32)
    scale = jnp.repeat(head_scale * (1.0 / math.log(2.0)), width // heads).reshape(1, width)
    group = (np.arange(tokens) // WW) % WH < half_lat
    same = np.tile(group[:, None] == group[None, :], (1, GROUP))
    mask = jnp.asarray(np.stack([np.ones_like(same), same]), BF16)
    lane_head = np.arange(256) // HEAD
    ones = jnp.asarray(lane_head[:, None] == lane_head[None, :], BF16)
    lane = jnp.asarray(np.arange(GROUP)[:, None] == lane_head[None, : GROUP * HEAD], BF16)
    sums = jnp.asarray(
        np.repeat(np.arange(GROUP), tokens)[:, None] == lane_head[None, : GROUP * HEAD], BF16
    )
    return run_kernel(
        functools.partial(front_body, half_lat),
        "front",
        [SCALARS] + [WHOLE] * 8 + [LEFT_OUT] + [WHOLE] * 4,
        [
            shaped((levels, rows, cols, width), BF16),
            shaped((coarse_tokens, 4 * width), BF16),
            shaped((coarse_tokens, coarse_width), BF16),
            shaped((coarse_tokens, coarse_width), BF16),
        ],
        [
            pltpu.VMEM((levels, ext_rows, cols + 16, width), F32),
            pltpu.VMEM((wins * tokens, width), F32),
            pltpu.VMEM((wins * tokens, 3 * width), BF16),
            pltpu.VMEM((wins * tokens, width), BF16),
            pltpu.VMEM((coarse_tokens, 4 * width), F32),
            pltpu.VMEM((coarse_tokens, 4 * width), BF16),
            pltpu.VMEM((levels, rows, width // LANES, cols, LANES), F32),
            pltpu.VMEM(merge_weight.shape, BF16),
            pltpu.SemaphoreType.DMA,
        ],
        30_000_000_000,
        12_000_000,
        flags, fine, top, bot, left, right, scale, qkv_weight, out_weight, merge_weight,
        mask, ones, lane, sums,
    )


def relative_place(dims, order, place_ref, block):
    strides = lon_strides(dims)
    at = 0
    for digit in order:
        n = dims[digit]
        d = (block // strides[digit]) % n
        at = at * n + lax.rem(d - place_ref[digit] + n, n)
    return at


def prep_body(dims, up_order, down_order, place_ref, *refs):
    n_up, n_down = dims[up_order[2]], dims[down_order[2]]
    up_parts, refs = refs[:n_up], refs[n_up:]
    down_parts, refs = refs[:n_down], refs[n_down:]
    cots, (up_ref, down_ref, grad_ref) = refs[:4], refs[4:]
    strides = lon_strides(dims)
    for parts, order, dest in ((up_parts, up_order, up_ref), (down_parts, down_order, down_ref)):
        first, mid, last = order
        depth = parts[0].shape[1]
        for k_last in range(dims[last]):
            for k_mid in range(dims[mid]):
                for k_first in range(dims[first]):
                    block = 0
                    for digit, k in ((first, k_first), (mid, k_mid), (last, k_last)):
                        block += lax.rem(place_ref[digit] + k, dims[digit]) * strides[digit]
                    piece = parts[k_last][k_mid * dims[first] + k_first]
                    dest[pl.ds(pl.multiple_of(block * depth, depth), depth), :] = piece
    for j in range(4):
        n = cots[j].shape[0]
        grad_ref[j * n : (j + 1) * n, :] = dot_nn(cots[j][...], down_ref[...]).astype(BF16)


def prep(place, up_parts, down_parts, cots, up_order, down_order, dims):
    ff = up_parts[0].shape[2]
    tokens, width = cots[0].shape
    return run_kernel(
        functools.partial(prep_body, dims, up_order, down_order),
        "prep",
        [SCALARS] + [WHOLE] * (len(up_parts) + len(down_parts) + 4),
        [shaped((width, ff), BF16), shaped((width, ff), BF16), shaped((4 * tokens, ff), BF16)],
        [],
        8 * tokens * width * ff,
        12_000_000,
        place, *up_parts, *down_parts, *cots,
    )


def feed_body(first_ref, second_ref, grad_ref, up_ref, down_ref, hid_ref, pre_ref, out_ref, back_ref):
    n, width = first_ref.shape
    ff = up_ref.shape[1]
    chunk = 256
    for j, tokens in enumerate((first_ref, second_ref)):
        at = slice(j * n, (j + 1) * n)
        for s in range(0, ff, chunk):
            pre = dot_nn(tokens[...], up_ref[:, s : s + chunk])
            cdf = 0.5 + 0.5 * lax.erf(pre * math.sqrt(0.5))
            hid_ref[at, s : s + chunk] = (pre * cdf).astype(BF16)
            slope = cdf + pre * (jnp.exp(-0.5 * (pre * pre)) * (1.0 / math.sqrt(2.0 * math.pi)))
            pre_ref[at, s : s + chunk] = (grad_ref[at, s : s + chunk].astype(F32) * slope).astype(BF16)
        back_ref[j] = dot_nt(pre_ref[at, :], up_ref[...]).astype(BF16)
        out_ref[j] = dot_nt(hid_ref[at, :], down_ref[...]).astype(BF16)


def feed(first, second, grads, up, down):
    n, width = first.shape
    ff = up.shape[1]
    return run_kernel(
        feed_body,
        "feed",
        [WHOLE] * 5,
        [
            shaped((2 * n, ff), BF16),
            shaped((2 * n, ff), BF16),
            shaped((2, n, width), BF16),
            shaped((2, n, width), BF16),
        ],
        [],
        12 * n * width * ff,
        10_000_000,
        first, second, grads, up, down,
    )


def term_body(dims, order, place_ref, *refs):
    lefts, rights, out_ref = refs[:4], refs[4:6], refs[6]
    n, width = lefts[0].shape
    blocks, depth, ff = out_ref.shape
    chunk = 256
    for s in range(0, width, chunk):
        total = None
        for j in range(4):
            right = rights[j // 2][(j % 2) * n : (j % 2 + 1) * n, :]
            term = dot_tn(lefts[j][:, s : s + chunk], right)
            total = term if total is None else total + term
        total = total.astype(BF16)
        per = max(1, chunk // depth)
        size = min(chunk, depth)
        for m in range(per):
            row = s + m * size
            at = relative_place(dims, order, place_ref, row // depth)
            inside = row % depth
            out_ref[at, inside : inside + size, :] = total[m * size : (m + 1) * size, :]


def term(place, lefts, rights, order, dims):
    n, width = lefts[0].shape
    ff = rights[0].shape[1]
    blocks = dims[0] * dims[1] * dims[2]
    return run_kernel(
        functools.partial(term_body, dims, order),
        "term",
        [SCALARS] + [WHOLE] * 6,
        [shaped((blocks, width // blocks, ff), BF16)],
        [],
        8 * n * width * ff,
        7_000_000,
        place, *lefts, *rights,
    )[0]


def last_body(coarse_ref, cot_ref, own_ref, there_ref, far_ref, cat_ref, merge_ref, skip_grad, slots, spread):
    levels, rows, cols, width = skip_grad.shape
    coarse = coarse_ref[...].astype(F32)
    normed, inverse = centre_scale(coarse)
    grad = own_ref[...].astype(F32) + there_ref[...].astype(F32) + far_ref[...].astype(F32)
    back = inverse * (
        grad
        - jnp.mean(grad, -1, keepdims=True)
        - normed * jnp.mean(grad * normed, -1, keepdims=True)
    )
    coarse_grad = (cot_ref[...].astype(F32) + back).astype(BF16)
    slots[...] = dot_nt(coarse_grad, merge_ref[...])
    half = cols // 2
    step = 96
    for s in range(0, slots.shape[0], step):
        normed, inverse = centre_scale(cat_ref[s : s + step, :].astype(F32))
        grad = slots[s : s + step, :]
        slots[s : s + step, :] = inverse * (
            grad
            - jnp.mean(grad, -1, keepdims=True)
            - normed * jnp.mean(grad * normed, -1, keepdims=True)
        )
    for l in range(levels):
        for i in range(rows // 2):
            at = (l * (rows // 2) + i) * half
            for a in range(2):
                for b in range(2):
                    for q in range(width // LANES):
                        to = (a + 2 * b) * width + q * LANES
                        spread[l, 2 * i + a, q, pl.ds(b, half, 2), :] = slots[
                            at : at + half, to : to + LANES
                        ]

    def lay_out(row, carry):
        for l in range(levels):
            for q in range(width // LANES):
                skip_grad[l, row, :, q * LANES : (q + 1) * LANES] = spread[l, row, q]
        return carry

    lax.fori_loop(0, rows, lay_out, 0)


def last(coarse, cot, own, there, far, cat, merge_weight, fine_shape):
    levels, rows, cols, width = fine_shape
    return run_kernel(
        last_body,
        "last",
        [WHOLE] * 7,
        [shaped(fine_shape, F32)],
        [
            pltpu.VMEM(cat.shape, F32),
            pltpu.VMEM((levels, rows, width // LANES, cols, LANES), F32),
        ],
        2 * cat.shape[0] * merge_weight.shape[0] * merge_weight.shape[1],
        10_000_000,
        coarse, cot, own, there, far, cat, merge_weight,
    )[0]


def with_rows(cells, width):
    count = lax.axis_size("lat")
    above = lax.ppermute(
        cells[:, -width:], "lat", [(i, (i + 1) % count) for i in range(count)]
    )
    below = lax.ppermute(cells[:, :width], "lat", [((i + 1) % count, i) for i in range(count)])
    return above, below


def on_device(
    fine_field, head_scale, qkv_weight, out_weight, merge_weight, up_weight, down_weight, cotangent
):
    levels, lat_rows, lon_cols, channels = fine_field.shape
    coarse_width = merge_weight.shape[1]
    half_lat, half_lon = WH // 2, WW // 2
    lon_count = lax.axis_size("lon")
    dims = lon_dims(lon_count)
    strides = lon_strides(dims)
    me = lax.axis_index("lon")
    place = jnp.stack([(me // strides[d]) % dims[d] for d in range(3)]).astype(jnp.int32)
    up_order, down_order = (0, 2, 1), (0, 1, 2)

    top, bot = with_rows(fine_field, half_lat)
    tall = [
        jnp.concatenate([top[:, :, cut], fine_field[:, :, cut], bot[:, :, cut]], 1)
        for cut in (slice(lon_cols - half_lon, lon_cols), slice(0, half_lon))
    ]
    left = lax.ppermute(tall[0], "lon", [(i, (i + 1) % lon_count) for i in range(lon_count)])
    right = lax.ppermute(tall[1], "lon", [((i + 1) % lon_count, i) for i in range(lon_count)])

    up_parts = gather_lon(up_weight, up_order)
    down_parts = gather_lon(down_weight.T, down_order)
    cot = cotangent.reshape(-1, coarse_width)
    cot_y = lat_swap(cot, 2)
    cots = [cot, lat_swap(cot, 1), cot_y, lat_swap(cot_y, 1)]

    skip_field, cat, coarse, normed = front(
        fine_field, top, bot, left, right, head_scale, qkv_weight, out_weight, merge_weight
    )
    normed_y = lat_swap(normed, 2)
    tokens = [normed, lat_swap(normed, 1), normed_y, lat_swap(normed_y, 1)]
    up, down, hidden_grad = prep(place, up_parts, down_parts, cots, up_order, down_order, dims)
    n = normed.shape[0]
    near = feed(tokens[0], tokens[1], hidden_grad[: 2 * n], up, down)
    away = feed(tokens[2], tokens[3], hidden_grad[2 * n :], up, down)

    def lat_sum(near_part, away_part):
        mine = away_part[0].astype(F32) + lat_swap(away_part[1], 1).astype(F32)
        return near_part[0], lat_swap(near_part[1], 1), lat_swap(mine.astype(BF16), 2)

    back_sums = lat_sum(near[3], away[3])
    out_sums = lat_sum(near[2], away[2])
    term_up = term(place, tokens, (near[1], away[1]), up_order[::-1], dims)
    term_down = term(place, cots, (near[0], away[0]), down_order[::-1], dims)
    up_grad = reduce_lon(term_up, up_order[::-1])
    down_grad = reduce_lon(term_down, down_order[::-1]).T
    coarse_out = (
        coarse.astype(F32)
        + (out_sums[0].astype(F32) + out_sums[1].astype(F32) + out_sums[2].astype(F32))
    ).astype(BF16)
    skip_grad = last(coarse, cot, *back_sums, cat, merge_weight, fine_field.shape)
    return (
        skip_field,
        coarse_out.reshape(levels, lat_rows // 2, lon_cols // 2, coarse_width),
        up_grad,
        down_grad,
        skip_grad,
    )


def solution(mesh):
    placed = (
        P(None, "lat", "lon", None),
        P(),
        P(),
        P(),
        P(),
        P("lon", "lat"),
        P("lat", "lon"),
        P(None, "lat", "lon", None),
    )
    return jax.shard_map(
        on_device,
        mesh=mesh,
        in_specs=placed,
        out_specs=(
            P(None, "lat", "lon", None),
            P(None, "lat", "lon", None),
            P("lon", "lat"),
            P("lat", "lon"),
            P(None, "lat", "lon", None),
        ),
        check_vma=False,
    )
```

```python
import functools
import math

import jax
import jax.numpy as jnp
import numpy as np
from jax import lax
from jax.experimental import pallas as pl
from jax.experimental.pallas import tpu as pltpu
from jax.sharding import PartitionSpec as P

WH = 6
WW = 12
HEAD = 32
LANES = 128
GROUP = 4
F32 = jnp.float32
BF16 = jnp.bfloat16
VMEM_BYTES = 56 * 1024 * 1024

WHOLE = pl.BlockSpec(memory_space=pltpu.VMEM)
SCALARS = pl.BlockSpec(memory_space=pltpu.SMEM)
LEFT_OUT = pl.BlockSpec(memory_space=pl.ANY)


def run_kernel(body, name, specs, outs, scratch, flops, moved, *operands):
    return pl.pallas_call(
        body,
        name=name,
        in_specs=specs,
        out_specs=[WHOLE] * len(outs),
        out_shape=outs,
        scratch_shapes=scratch,
        compiler_params=pltpu.CompilerParams(vmem_limit_bytes=VMEM_BYTES),
        cost_estimate=pl.CostEstimate(flops=1000, bytes_accessed=1000, transcendentals=0),
    )(*operands)


def shaped(shape, kind):
    return jax.ShapeDtypeStruct(shape, kind)


def dot_nn(left, right):
    return lax.dot_general(left, right, (((1,), (0,)), ((), ())), preferred_element_type=F32)


def dot_nt(left, right):
    return lax.dot_general(left, right, (((1,), (1,)), ((), ())), preferred_element_type=F32)


def dot_tn(left, right):
    return lax.dot_general(left, right, (((0,), (0,)), ((), ())), preferred_element_type=F32)


def centre_scale(rows):
    centred = rows - jnp.mean(rows, -1, keepdims=True)
    inverse = lax.rsqrt(jnp.mean(centred * centred, -1, keepdims=True) + 1e-05)
    return centred * inverse, inverse


DIMS = (2, 4, 4)
STRIDES = (16, 4, 1)


def lat_swap(array, bits):
    count = lax.axis_size("lat")
    return lax.ppermute(array, "lat", [(i, i ^ bits) for i in range(count)])


def lon_swap(array, digit, bits):
    count = lax.axis_size("lon")
    return lax.ppermute(array, "lon", [(i, i ^ (bits * STRIDES[digit])) for i in range(count)])


def add_parts(*arrays):
    return sum(array.astype(F32) for array in arrays).astype(BF16)


def gather_mid(own, digit):
    pair = jnp.stack([own, lon_swap(own, digit, 1)])
    return pair, lon_swap(pair, digit, 3)


def gather_near(stacks, digit):
    first, second = stacks
    return (
        jnp.stack([first, lon_swap(first, digit, 1)]),
        jnp.stack([second, lon_swap(second, digit, 3)]),
    )


def gather_far(near, digit):
    return lon_swap(near[0], digit, 3), lon_swap(near[1], digit, 1)


def front_body(
    half_lat, flag_ref, x_ref, top_ref, bot_ref, left_ref, right_ref, scale_ref, qkv_w, out_w,
    merge_hbm, mask_ref, ones_ref, lane_ref, sums_ref, *refs,
):
    (
        skip_ref, cat_ref, coarse_ref, normed_ref,
        ext, xw, qkv, att, cat, catn, spread, merge_w, sem,
    ) = refs[-13:]
    levels, rows, cols, width = x_ref.shape
    fetch = pltpu.make_async_copy(merge_hbm, merge_w, sem)
    fetch.start()
    lead = 8
    half_lon = left_ref.shape[2]
    tokens = levels * WH * WW
    wins = (cols + 2 * half_lon) // WW

    def fill(row, carry):
        for l in range(levels):
            ext[l, half_lat + row, lead : lead + cols, :] = x_ref[l, row].astype(F32)
        return carry

    lax.fori_loop(0, rows, fill, 0)
    for l in range(levels):
        for r in range(half_lat):
            ext[l, r, lead : lead + cols, :] = top_ref[l, r].astype(F32)
            ext[l, half_lat + rows + r, lead : lead + cols, :] = bot_ref[l, r].astype(F32)

    def fill_sides(row, carry):
        for l in range(levels):
            ext[l, row, lead - half_lon : lead, :] = left_ref[l, row].astype(F32)
            ext[l, row, lead + cols : lead + cols + half_lon, :] = right_ref[l, row].astype(F32)
        return carry

    lax.fori_loop(0, rows + 2 * half_lat, fill_sides, 0)

    chunk = 256
    sections = width // chunk
    groups = width // (GROUP * HEAD)
    lanes = GROUP * HEAD

    def places():
        for c in range(wins):
            for l in range(levels):
                for r in range(WH):
                    yield c, l, r

    def band(b, carry):
        for c, l, r in places():
            at = c * tokens + (l * WH + r) * WW
            start = lead - half_lon + c * WW
            xw[at : at + WW, :] = ext[l, b * WH + r, start : start + WW, :]
        normed = centre_scale(xw[...])[0].astype(BF16)
        for j in range(3 * sections):
            y = dot_nn(normed, qkv_w[:, j * chunk : (j + 1) * chunk])
            if j < 2 * sections:
                square = y * y
                high = square.astype(BF16)
                low = (square - high.astype(F32)).astype(BF16)
                total = dot_nn(high, ones_ref[...]) + dot_nn(low, ones_ref[...])
                y = y * lax.rsqrt(total + 1e-06)
                if j < sections:
                    y = y * scale_ref[:, j * chunk : (j + 1) * chunk]
            qkv[:, j * chunk : (j + 1) * chunk] = y.astype(BF16)
        allowed = mask_ref[flag_ref[b]]
        for c in range(wins):
            rows_at = slice(c * tokens, (c + 1) * tokens)
            for g in range(groups):
                q = qkv[rows_at, g * lanes : (g + 1) * lanes]
                k = qkv[rows_at, width + g * lanes : width + (g + 1) * lanes]
                v = qkv[rows_at, 2 * width + g * lanes : 2 * width + (g + 1) * lanes]
                k4 = jnp.concatenate([k * lane_ref[h : h + 1, :] for h in range(GROUP)], 0)
                v4 = jnp.concatenate([v * lane_ref[h : h + 1, :] for h in range(GROUP)], 0)
                weight = jnp.exp2(dot_nt(q, k4)).astype(BF16) * allowed
                both = dot_nn(weight, jnp.concatenate([v4, sums_ref[...]], 1))
                att[rows_at, g * lanes : (g + 1) * lanes] = (
                    both[:, :lanes] / both[:, lanes:]
                ).astype(BF16)
        skip = xw[...] + dot_nn(att[...], out_w[...])
        xw[...] = skip.astype(BF16).astype(F32)
        for c, l, r in places():
            at = c * tokens + (l * WH + r) * WW
            start = lead - half_lon + c * WW
            ext[l, b * WH + r, start : start + WW, :] = xw[at : at + WW, :]
        return carry

    lax.fori_loop(0, (rows + 2 * half_lat) // WH, band, 0)

    def store_skip(row, carry):
        for l in range(levels):
            line = ext[l, half_lat + row, lead : lead + cols, :]
            skip_ref[l, row] = line.astype(BF16)
            for q in range(width // LANES):
                spread[l, row, q] = line[:, q * LANES : (q + 1) * LANES]
        return carry

    lax.fori_loop(0, rows, store_skip, 0)
    half = cols // 2
    for l in range(levels):
        for i in range(rows // 2):
            at = (l * (rows // 2) + i) * half
            for a in range(2):
                for b in range(2):
                    for q in range(width // LANES):
                        to = (a + 2 * b) * width + q * LANES
                        cat[at : at + half, to : to + LANES] = spread[
                            l, 2 * i + a, q, pl.ds(b, half, 2), :
                        ]
    total = cat.shape[0]
    step = 96
    for s in range(0, total, step):
        piece = cat[s : s + step, :]
        cat_ref[s : s + step, :] = piece.astype(BF16)
        catn[s : s + step, :] = centre_scale(piece)[0].astype(BF16)
    fetch.wait()
    coarse = dot_nn(catn[...], merge_w[...]).astype(BF16)
    coarse_ref[...] = coarse
    normed_ref[...] = centre_scale(coarse.astype(F32))[0].astype(BF16)


def front(fine, top, bot, left, right, head_scale, qkv_weight, out_weight, merge_weight, after):
    levels, rows, cols, width = fine.shape
    half_lat = WH // 2
    tokens = levels * WH * WW
    ext_rows = rows + 2 * half_lat
    bands = ext_rows // WH
    wins = (cols + WW) // WW
    heads = head_scale.shape[0]
    coarse_width = merge_weight.shape[1]
    coarse_tokens = levels * rows * cols // 4
    lat_place = lax.axis_index("lat")
    lat_last = lax.axis_size("lat") - 1
    band_ids = jnp.arange(bands)
    flags = (
        ((band_ids == 0) & (lat_place == 0)) | ((band_ids == bands - 1) & (lat_place == lat_last))
    ).astype(jnp.int32)
    scale = jnp.repeat(head_scale * (1.0 / math.log(2.0)), width // heads).reshape(1, width)
    group = (np.arange(tokens) // WW) % WH < half_lat
    same = np.tile(group[:, None] == group[None, :], (1, GROUP))
    mask = jnp.asarray(np.stack([np.ones_like(same), same]), BF16)
    lane_head = np.arange(256) // HEAD
    ones = jnp.asarray(lane_head[:, None] == lane_head[None, :], BF16)
    lane = jnp.asarray(np.arange(GROUP)[:, None] == lane_head[None, : GROUP * HEAD], BF16)
    sums = jnp.asarray(
        np.repeat(np.arange(GROUP), tokens)[:, None] == lane_head[None, : GROUP * HEAD], BF16
    )
    return run_kernel(
        functools.partial(front_body, half_lat),
        "front",
        [SCALARS] + [WHOLE] * 8 + [LEFT_OUT] + [WHOLE] * 4 + [LEFT_OUT] * len(after),
        [
            shaped((levels, rows, cols, width), BF16),
            shaped((coarse_tokens, 4 * width), BF16),
            shaped((coarse_tokens, coarse_width), BF16),
            shaped((coarse_tokens, coarse_width), BF16),
        ],
        [
            pltpu.VMEM((levels, ext_rows, cols + 16, width), F32),
            pltpu.VMEM((wins * tokens, width), F32),
            pltpu.VMEM((wins * tokens, 3 * width), BF16),
            pltpu.VMEM((wins * tokens, width), BF16),
            pltpu.VMEM((coarse_tokens, 4 * width), F32),
            pltpu.VMEM((coarse_tokens, 4 * width), BF16),
            pltpu.VMEM((levels, rows, width // LANES, cols, LANES), F32),
            pltpu.VMEM(merge_weight.shape, BF16),
            pltpu.SemaphoreType.DMA,
        ],
        30_000_000_000,
        12_000_000,
        flags, fine, top, bot, left, right, scale, qkv_weight, out_weight, merge_weight,
        mask, ones, lane, sums, *after,
    )


def lay_blocks(place_ref, mid, last, near, far, dest):
    depth = dest.shape[0] // (DIMS[0] * DIMS[1] * DIMS[2])
    for stack, (mids, lasts) in enumerate((((0, 1), (0, 1, 3, 2)), ((3, 2), (0, 3, 1, 2)))):
        for at, k_last in enumerate(lasts):
            ref = near[stack] if at < 2 else far[stack]
            for m, k_mid in enumerate(mids):
                for k_first in range(DIMS[0]):
                    block = 0
                    for digit, k in ((0, k_first), (mid, k_mid), (last, k_last)):
                        block += jnp.bitwise_xor(place_ref[digit], k) * STRIDES[digit]
                    start = pl.multiple_of(block * depth, depth)
                    dest[pl.ds(start, depth), :] = ref[at % 2, m, k_first]


def prep_body(place_ref, *refs):
    up_parts, down_parts, cots = refs[:4], refs[4:8], refs[8:12]
    up_ref, up_t_ref, down_ref, near_ref, away_ref, down_t = refs[12:]
    lay_blocks(place_ref, 2, 1, up_parts[:2], up_parts[2:], up_ref)
    lay_blocks(place_ref, 1, 2, down_parts[:2], down_parts[2:], down_t)
    for j in range(4):
        n = cots[j].shape[0]
        grad_ref = near_ref if j < 2 else away_ref
        at = slice((j % 2) * n, (j % 2 + 1) * n)
        grad_ref[at, :] = dot_nn(cots[j][...], down_t[...]).astype(BF16)
    ff = up_ref.shape[1]
    step = 256
    for s in range(0, ff, step):
        up_t_ref[s : s + step, :] = up_ref[:, s : s + step].T
        down_ref[s : s + step, :] = down_t[:, s : s + step].T


def prep(place, up_parts, down_parts, cots):
    ff = up_parts[0].shape[-1]
    tokens, width = cots[0].shape
    return run_kernel(
        prep_body,
        "prep",
        [SCALARS] + [WHOLE] * 12,
        [
            shaped((width, ff), BF16),
            shaped((ff, width), BF16),
            shaped((ff, width), BF16),
            shaped((2 * tokens, ff), BF16),
            shaped((2 * tokens, ff), BF16),
        ],
        [pltpu.VMEM((width, ff), BF16)],
        8 * tokens * width * ff,
        12_000_000,
        place, *up_parts, *down_parts, *cots,
    )


TERM_PARTS = (((0, 3), (0, 3)), ((1, 2), (0, 3)), ((0, 1), (1, 2)), ((3, 2), (1, 2)))


def term_into(held, place_ref, left, right, mid, last):
    width = left.shape[1]
    depth = held.shape[3]
    chunk = 256
    for s in range(0, width, chunk):
        total = dot_tn(left[:, s : s + chunk], right[...]).astype(BF16)
        for m in range(chunk // depth):
            block = s // depth + m
            k = [
                jnp.bitwise_xor(place_ref[digit], (block // STRIDES[digit]) % DIMS[digit])
                for digit in range(3)
            ]
            held[k[last], k[mid], k[0]] = total[m * depth : (m + 1) * depth, :]


def feed_body(place_ref, *refs):
    token_refs, cot_refs, grad_refs, refs = refs[:4], refs[4:8], refs[8:10], refs[10:]
    (up_hbm, up_t_hbm, down_hbm), refs = refs[:3], refs[3:]
    up_outs, down_outs, (near_hbm, away_hbm, send_hbm), refs = refs[:4], refs[4:8], refs[8:11], refs[11:]
    tok, cot, grads, up, up_t, down, hid, pre, held_u, held_d, near, away, send, ins, outs = refs
    n = token_refs[0].shape[0]
    ff = up.shape[1]
    pairs = [(up_hbm, up)]
    for h in range(2):
        pairs += [(token_refs[j], tok.at[pl.ds(j * n, n)]) for j in (2 * h, 2 * h + 1)]
        pairs += [(grad_refs[h], grads.at[pl.ds(2 * h * n, 2 * n)])]
    pairs += [(cot_refs[j], cot.at[pl.ds(j * n, n)]) for j in range(4)]
    pairs += [(up_t_hbm, up_t), (down_hbm, down)]
    fetches = [pltpu.make_async_copy(a, b, ins.at[i]) for i, (a, b) in enumerate(pairs)]
    for fetch in fetches:
        fetch.start()
    stores = []

    def store(src, dst):
        copy = pltpu.make_async_copy(src, dst, outs.at[len(stores)])
        copy.start()
        stores.append(copy)

    fetches[0].wait()
    chunk = 256
    for j in range(4):
        if j % 2 == 0:
            for k in range(3):
                fetches[1 + 3 * (j // 2) + k].wait()
        at = slice(j * n, (j + 1) * n)
        for s in range(0, ff, chunk):
            act = dot_nn(tok[at, :], up[:, s : s + chunk])
            cdf = 0.5 + 0.5 * lax.erf(act * math.sqrt(0.5))
            hid[at, s : s + chunk] = (act * cdf).astype(BF16)
            slope = cdf + act * (jnp.exp(-0.5 * (act * act)) * (1.0 / math.sqrt(2.0 * math.pi)))
            pre[at, s : s + chunk] = (
                grads[at, s : s + chunk].astype(F32) * slope
            ).astype(BF16)
    for k in range(7, 11):
        fetches[k].wait()
    for held, left, right, parts, mid, last in (
        (held_d, cot, hid, down_outs, 1, 2),
        (held_u, tok, pre, up_outs, 2, 1),
    ):
        term_into(held, place_ref, left, right, mid, last)
        for out, (lasts, mids) in zip(parts, TERM_PARTS):
            for i, k_last in enumerate(lasts):
                for m, k_mid in enumerate(mids):
                    store(held.at[k_last, k_mid], out.at[i, m])
    for which, (rows, weight) in enumerate(((pre, up_t), (hid, down))):
        fetches[11 + which].wait()
        for side, (keep, keep_hbm) in enumerate(((near, near_hbm), (away, away_hbm))):
            sums = dot_nn(rows[2 * side * n : 2 * (side + 1) * n, :], weight[...]).astype(BF16)
            keep[which] = sums[:n]
            send[2 * side + which] = sums[n:]
            store(keep.at[which], keep_hbm.at[which])
            store(send.at[2 * side + which], send_hbm.at[2 * side + which])
    for copy in stores:
        copy.wait()


def feed(place, tokens, cots, grads, up, up_t, down):
    n, width = tokens[0].shape
    ff = up.shape[1]
    depth = width // (DIMS[0] * DIMS[1] * DIMS[2])
    part = shaped((2, 2, DIMS[0], depth, ff), BF16)
    outs = [part] * 8 + [shaped((k, n, width), BF16) for k in (2, 2, 4)]
    result = pl.pallas_call(
        feed_body,
        name="feed",
        in_specs=[SCALARS] + [LEFT_OUT] * 13,
        out_specs=[LEFT_OUT] * len(outs),
        out_shape=outs,
        scratch_shapes=[
            pltpu.VMEM((4 * n, width), BF16),
            pltpu.VMEM((4 * n, width), BF16),
            pltpu.VMEM((4 * n, ff), BF16),
            pltpu.VMEM((width, ff), BF16),
            pltpu.VMEM((ff, width), BF16),
            pltpu.VMEM((ff, width), BF16),
            pltpu.VMEM((4 * n, ff), BF16),
            pltpu.VMEM((4 * n, ff), BF16),
            pltpu.VMEM((4, 4, DIMS[0], depth, ff), BF16),
            pltpu.VMEM((4, 4, DIMS[0], depth, ff), BF16),
            pltpu.VMEM((2, n, width), BF16),
            pltpu.VMEM((2, n, width), BF16),
            pltpu.VMEM((4, n, width), BF16),
            pltpu.SemaphoreType.DMA((13,)),
            pltpu.SemaphoreType.DMA((40,)),
        ],
        compiler_params=pltpu.CompilerParams(vmem_limit_bytes=VMEM_BYTES),
        cost_estimate=pl.CostEstimate(flops=1000, bytes_accessed=1000, transcendentals=0),
    )(place, *tokens, *cots, *grads, up, up_t, down)
    return result[:4], result[4:8], result[8:]


def last_body(coarse_ref, cot_ref, own_ref, there_ref, far_ref, cat_ref, merge_ref, *refs):
    skip_grad, slots, spread, shares, sems = refs[-5:]
    fetches = [
        pltpu.make_async_copy(ref.at[0], shares.at[k], sems.at[k])
        for k, ref in enumerate((own_ref, there_ref))
    ]
    for fetch in fetches:
        fetch.start()
    levels, rows, cols, width = skip_grad.shape
    coarse = coarse_ref[...].astype(F32)
    normed, inverse = centre_scale(coarse)
    for fetch in fetches:
        fetch.wait()
    grad = shares[0].astype(F32) + shares[1].astype(F32) + far_ref[...].astype(F32)
    back = inverse * (
        grad
        - jnp.mean(grad, -1, keepdims=True)
        - normed * jnp.mean(grad * normed, -1, keepdims=True)
    )
    coarse_grad = (cot_ref[...].astype(F32) + back).astype(BF16)
    slots[...] = dot_nt(coarse_grad, merge_ref[...])
    half = cols // 2
    step = 96
    for s in range(0, slots.shape[0], step):
        normed, inverse = centre_scale(cat_ref[s : s + step, :].astype(F32))
        grad = slots[s : s + step, :]
        slots[s : s + step, :] = inverse * (
            grad
            - jnp.mean(grad, -1, keepdims=True)
            - normed * jnp.mean(grad * normed, -1, keepdims=True)
        )
    for l in range(levels):
        for i in range(rows // 2):
            at = (l * (rows // 2) + i) * half
            for a in range(2):
                for b in range(2):
                    for q in range(width // LANES):
                        to = (a + 2 * b) * width + q * LANES
                        spread[l, 2 * i + a, q, pl.ds(b, half, 2), :] = slots[
                            at : at + half, to : to + LANES
                        ]

    def lay_out(row, carry):
        for l in range(levels):
            for q in range(width // LANES):
                skip_grad[l, row, :, q * LANES : (q + 1) * LANES] = spread[l, row, q]
        return carry

    lax.fori_loop(0, rows, lay_out, 0)


def last(coarse, cot, own, there, far, cat, merge_weight, fine_shape, after):
    levels, rows, cols, width = fine_shape
    return run_kernel(
        last_body,
        "last",
        [WHOLE] * 2 + [LEFT_OUT] * 2 + [WHOLE] * 3 + [LEFT_OUT] * len(after),
        [shaped(fine_shape, F32)],
        [
            pltpu.VMEM(cat.shape, F32),
            pltpu.VMEM((levels, rows, width // LANES, cols, LANES), F32),
            pltpu.VMEM((2, *own.shape[1:]), BF16),
            pltpu.SemaphoreType.DMA((2,)),
        ],
        2 * cat.shape[0] * merge_weight.shape[0] * merge_weight.shape[1],
        10_000_000,
        coarse, cot, own, there, far, cat, merge_weight, *after,
    )[0]


def with_rows(cells, width):
    count = lax.axis_size("lat")
    above = lax.ppermute(
        cells[:, -width:], "lat", [(i, (i + 1) % count) for i in range(count)]
    )
    below = lax.ppermute(cells[:, :width], "lat", [((i + 1) % count, i) for i in range(count)])
    return above, below


def on_device(
    fine_field, head_scale, qkv_weight, out_weight, merge_weight, up_weight, down_weight, cotangent
):
    levels, lat_rows, lon_cols, channels = fine_field.shape
    coarse_width = merge_weight.shape[1]
    half_lat, half_lon = WH // 2, WW // 2
    lon_count = lax.axis_size("lon")
    me = lax.axis_index("lon")
    place = jnp.stack([(me // STRIDES[d]) % DIMS[d] for d in range(3)]).astype(jnp.int32)

    weights = jnp.stack([up_weight, down_weight.T])[:, None]
    weights = jnp.concatenate([weights, lon_swap(weights, 0, 1)], 1)
    top, bot = with_rows(fine_field, half_lat)
    tall = [
        jnp.concatenate([top[:, :, cut], fine_field[:, :, cut], bot[:, :, cut]], 1)
        for cut in (slice(lon_cols - half_lon, lon_cols), slice(0, half_lon))
    ]
    left = lax.ppermute(tall[0], "lon", [(i, (i + 1) % lon_count) for i in range(lon_count)])
    right = lax.ppermute(tall[1], "lon", [((i + 1) % lon_count, i) for i in range(lon_count)])
    up_near = gather_near(gather_mid(weights[0], 2), 1)
    down_near = gather_near(gather_mid(weights[1], 1), 2)
    cot = cotangent.reshape(-1, coarse_width)
    held, _, _ = lax.optimization_barrier((cot, left, right))
    cot_c, cot_y = lat_swap(held, 1), lat_swap(held, 2)
    skip_field, cat, coarse, normed = front(
        fine_field, top, bot, left, right, head_scale, qkv_weight, out_weight, merge_weight,
        (*up_near, *down_near, cot_c),
    )
    up_far, down_far = gather_far(up_near, 1), gather_far(down_near, 2)
    normed, up_far, down_far, cot_y = lax.optimization_barrier((normed, up_far, down_far, cot_y))
    cots = [cot, cot_c, cot_y, lat_swap(cot_y, 1)]
    normed_c, normed_y = lat_swap(normed, 1), lat_swap(normed, 2)
    up, up_t, down, near_grad, away_grad = prep(
        place, (*up_near, *up_far), (*down_near, *down_far), cots
    )
    normed_y, normed_c, up = lax.optimization_barrier((normed_y, normed_c, up))
    tokens = [normed, normed_c, normed_y, lat_swap(normed_y, 1)]

    def scatter_one(parts, digit):
        return lon_swap(parts[1], digit, 1), lon_swap(parts[3], digit, 3)

    def scatter_two(parts, came, digit):
        keep = [add_parts(parts[2 * h][0], came[h][0]) for h in range(2)]
        send = [add_parts(parts[2 * h][1], came[h][1]) for h in range(2)]
        return keep, send, (lon_swap(send[0], digit, 3), lon_swap(send[1], digit, 1))

    term_up, term_down, (near, away, send) = feed(
        place, tokens, cots, (near_grad, away_grad), up, up_t, down
    )
    there = lat_swap(send, 1)
    up_came, down_came = scatter_one(term_up, 1), scatter_one(term_down, 2)
    back_pass = add_parts(away[0], there[2])
    back_far = lat_swap(back_pass, 2)
    up_came, down_came, back_pass = lax.optimization_barrier((up_came, down_came, back_pass))
    up_keep, _, up_came = scatter_two(term_up, up_came, 1)
    down_keep, _, down_came = scatter_two(term_down, down_came, 2)
    up_halves = [add_parts(up_keep[h], up_came[h]) for h in range(2)]
    down_halves = [add_parts(down_keep[h], down_came[h]) for h in range(2)]
    up_came, down_came = lon_swap(up_halves[1], 2, 1), lon_swap(down_halves[1], 1, 1)
    out_pass = add_parts(away[1], there[3])
    out_far = lat_swap(out_pass, 2)
    skip_grad = last(
        coarse, cot, near, there, back_far, cat, merge_weight, fine_field.shape,
        (up_halves[1], down_halves[1]),
    )
    up_came, down_came, skip_grad = lax.optimization_barrier((up_came, down_came, skip_grad))
    up_pair, down_pair = add_parts(up_halves[0], up_came), add_parts(down_halves[0], down_came)
    up_end = add_parts(up_pair[0], lon_swap(up_pair[1], 2, 3))
    down_end = add_parts(down_pair[0], lon_swap(down_pair[1], 1, 3))
    both = jnp.stack([up_end, down_end], 1)
    both = both[0].astype(F32) + lon_swap(both[1], 0, 1).astype(F32)
    coarse_out = (
        coarse.astype(F32)
        + (near[1].astype(F32) + there[1].astype(F32) + out_far.astype(F32))
    ).astype(BF16)
    return (
        skip_field,
        coarse_out.reshape(levels, lat_rows // 2, lon_cols // 2, coarse_width),
        both[0],
        both[1].T,
        skip_grad,
    )


def solution(mesh):
    placed = (
        P(None, "lat", "lon", None),
        P(),
        P(),
        P(),
        P(),
        P("lon", "lat"),
        P("lat", "lon"),
        P(None, "lat", "lon", None),
    )
    return jax.shard_map(
        on_device,
        mesh=mesh,
        in_specs=placed,
        out_specs=(
            P(None, "lat", "lon", None),
            P(None, "lat", "lon", None),
            P("lon", "lat"),
            P("lat", "lon"),
            P(None, "lat", "lon", None),
        ),
        check_vma=False,
    )
```

```python
import functools
import math

import jax
import jax.numpy as jnp
import numpy as np
from jax import lax
from jax.experimental import pallas as pl
from jax.experimental.pallas import tpu as pltpu
from jax.sharding import PartitionSpec as P

WH = 6
WW = 12
HEAD = 32
LANES = 128
GROUP = 4
F32 = jnp.float32
BF16 = jnp.bfloat16
MIB = 1024 * 1024

WHOLE = pl.BlockSpec(memory_space=pltpu.VMEM)
SCALARS = pl.BlockSpec(memory_space=pltpu.SMEM)
LEFT_OUT = pl.BlockSpec(memory_space=pl.ANY)


def run_kernel(body, name, specs, outs, scratch, flops, moved, *operands, vmem):
    return pl.pallas_call(
        body,
        name=name,
        in_specs=specs,
        out_specs=[WHOLE] * len(outs),
        out_shape=outs,
        scratch_shapes=scratch,
        compiler_params=pltpu.CompilerParams(vmem_limit_bytes=vmem),
        cost_estimate=pl.CostEstimate(flops=1000, bytes_accessed=1000, transcendentals=0),
    )(*operands)


def shaped(shape, kind):
    return jax.ShapeDtypeStruct(shape, kind)


def dot_nn(left, right):
    return lax.dot_general(left, right, (((1,), (0,)), ((), ())), preferred_element_type=F32)


def dot_nt(left, right):
    return lax.dot_general(left, right, (((1,), (1,)), ((), ())), preferred_element_type=F32)


def dot_tn(left, right):
    return lax.dot_general(left, right, (((0,), (0,)), ((), ())), preferred_element_type=F32)


def centre_scale(rows):
    centred = rows - jnp.mean(rows, -1, keepdims=True)
    inverse = lax.rsqrt(jnp.mean(centred * centred, -1, keepdims=True) + 1e-05)
    return centred * inverse, inverse


DIMS = (2, 4, 4)
STRIDES = (16, 4, 1)


def lat_swap(array, bits):
    count = lax.axis_size("lat")
    return lax.ppermute(array, "lat", [(i, i ^ bits) for i in range(count)])


def lon_swap(array, digit, bits):
    count = lax.axis_size("lon")
    return lax.ppermute(array, "lon", [(i, i ^ (bits * STRIDES[digit])) for i in range(count)])


def add_parts(*arrays):
    return sum(array.astype(F32) for array in arrays).astype(BF16)


def gather_mid(own, digit):
    pair = jnp.stack([own, lon_swap(own, digit, 1)])
    return pair, lon_swap(pair, digit, 3)


def gather_near(stacks, digit):
    first, second = stacks
    return (
        jnp.stack([first, lon_swap(first, digit, 1)]),
        jnp.stack([second, lon_swap(second, digit, 3)]),
    )


def gather_far(near, digit):
    return lon_swap(near[0], digit, 3), lon_swap(near[1], digit, 1)


def front_body(
    half_lat, flag_ref, x_ref, top_ref, bot_ref, left_ref, right_ref, scale_ref, qkv_w, out_w,
    merge_hbm, mask_ref, ones_ref, lane_ref, sums_ref, *refs,
):
    (
        skip_ref, cat_ref, coarse_ref, normed_ref,
        ext, xw, qkv, att, cat, catn, spread, merge_w, sem,
    ) = refs[-13:]
    levels, rows, cols, width = x_ref.shape
    fetch = pltpu.make_async_copy(merge_hbm, merge_w, sem)
    fetch.start()
    lead = 8
    half_lon = left_ref.shape[2]
    tokens = levels * WH * WW
    wins = (cols + 2 * half_lon) // WW

    def fill(row, carry):
        for l in range(levels):
            ext[l, half_lat + row, lead : lead + cols, :] = x_ref[l, row].astype(F32)
        return carry

    lax.fori_loop(0, rows, fill, 0)
    for l in range(levels):
        for r in range(half_lat):
            ext[l, r, lead : lead + cols, :] = top_ref[l, r].astype(F32)
            ext[l, half_lat + rows + r, lead : lead + cols, :] = bot_ref[l, r].astype(F32)

    def fill_sides(row, carry):
        for l in range(levels):
            ext[l, row, lead - half_lon : lead, :] = left_ref[l, row].astype(F32)
            ext[l, row, lead + cols : lead + cols + half_lon, :] = right_ref[l, row].astype(F32)
        return carry

    lax.fori_loop(0, rows + 2 * half_lat, fill_sides, 0)

    chunk = 256
    sections = width // chunk
    groups = width // (GROUP * HEAD)
    lanes = GROUP * HEAD

    def places():
        for c in range(wins):
            for l in range(levels):
                for r in range(WH):
                    yield c, l, r

    def band(b, carry):
        for c, l, r in places():
            at = c * tokens + (l * WH + r) * WW
            start = lead - half_lon + c * WW
            xw[at : at + WW, :] = ext[l, b * WH + r, start : start + WW, :]
        normed = centre_scale(xw[...])[0].astype(BF16)
        for j in range(3 * sections):
            y = dot_nn(normed, qkv_w[:, j * chunk : (j + 1) * chunk])
            if j < 2 * sections:
                square = y * y
                high = square.astype(BF16)
                low = (square - high.astype(F32)).astype(BF16)
                total = dot_nn(high, ones_ref[...]) + dot_nn(low, ones_ref[...])
                y = y * lax.rsqrt(total + 1e-06)
                if j < sections:
                    y = y * scale_ref[:, j * chunk : (j + 1) * chunk]
            qkv[:, j * chunk : (j + 1) * chunk] = y.astype(BF16)
        allowed = mask_ref[flag_ref[b]]
        for c in range(wins):
            rows_at = slice(c * tokens, (c + 1) * tokens)
            for g in range(groups):
                q = qkv[rows_at, g * lanes : (g + 1) * lanes]
                k = qkv[rows_at, width + g * lanes : width + (g + 1) * lanes]
                v = qkv[rows_at, 2 * width + g * lanes : 2 * width + (g + 1) * lanes]
                k4 = jnp.concatenate([k * lane_ref[h : h + 1, :] for h in range(GROUP)], 0)
                v4 = jnp.concatenate([v * lane_ref[h : h + 1, :] for h in range(GROUP)], 0)
                weight = jnp.exp2(dot_nt(q, k4)).astype(BF16) * allowed
                both = dot_nn(weight, jnp.concatenate([v4, sums_ref[...]], 1))
                att[rows_at, g * lanes : (g + 1) * lanes] = (
                    both[:, :lanes] / both[:, lanes:]
                ).astype(BF16)
        skip = xw[...] + dot_nn(att[...], out_w[...])
        xw[...] = skip.astype(BF16).astype(F32)
        for c, l, r in places():
            at = c * tokens + (l * WH + r) * WW
            start = lead - half_lon + c * WW
            ext[l, b * WH + r, start : start + WW, :] = xw[at : at + WW, :]
        return carry

    lax.fori_loop(0, (rows + 2 * half_lat) // WH, band, 0)

    def store_skip(row, carry):
        for l in range(levels):
            line = ext[l, half_lat + row, lead : lead + cols, :]
            skip_ref[l, row] = line.astype(BF16)
            for q in range(width // LANES):
                spread[l, row, q] = line[:, q * LANES : (q + 1) * LANES]
        return carry

    lax.fori_loop(0, rows, store_skip, 0)
    half = cols // 2
    for l in range(levels):
        for i in range(rows // 2):
            at = (l * (rows // 2) + i) * half
            for a in range(2):
                for b in range(2):
                    for q in range(width // LANES):
                        to = (a + 2 * b) * width + q * LANES
                        cat[at : at + half, to : to + LANES] = spread[
                            l, 2 * i + a, q, pl.ds(b, half, 2), :
                        ]
    total = cat.shape[0]
    step = 96
    for s in range(0, total, step):
        piece = cat[s : s + step, :]
        cat_ref[s : s + step, :] = piece.astype(BF16)
        catn[s : s + step, :] = centre_scale(piece)[0].astype(BF16)
    fetch.wait()
    coarse = dot_nn(catn[...], merge_w[...]).astype(BF16)
    coarse_ref[...] = coarse
    normed_ref[...] = centre_scale(coarse.astype(F32))[0].astype(BF16)


def front(fine, top, bot, left, right, head_scale, qkv_weight, out_weight, merge_weight, after):
    levels, rows, cols, width = fine.shape
    half_lat = WH // 2
    tokens = levels * WH * WW
    ext_rows = rows + 2 * half_lat
    bands = ext_rows // WH
    wins = (cols + WW) // WW
    heads = head_scale.shape[0]
    coarse_width = merge_weight.shape[1]
    coarse_tokens = levels * rows * cols // 4
    lat_place = lax.axis_index("lat")
    lat_last = lax.axis_size("lat") - 1
    band_ids = jnp.arange(bands)
    flags = (
        ((band_ids == 0) & (lat_place == 0)) | ((band_ids == bands - 1) & (lat_place == lat_last))
    ).astype(jnp.int32)
    scale = jnp.repeat(head_scale * (1.0 / math.log(2.0)), width // heads).reshape(1, width)
    group = (np.arange(tokens) // WW) % WH < half_lat
    same = np.tile(group[:, None] == group[None, :], (1, GROUP))
    mask = jnp.asarray(np.stack([np.ones_like(same), same]), BF16)
    lane_head = np.arange(256) // HEAD
    ones = jnp.asarray(lane_head[:, None] == lane_head[None, :], BF16)
    lane = jnp.asarray(np.arange(GROUP)[:, None] == lane_head[None, : GROUP * HEAD], BF16)
    sums = jnp.asarray(
        np.repeat(np.arange(GROUP), tokens)[:, None] == lane_head[None, : GROUP * HEAD], BF16
    )
    return run_kernel(
        functools.partial(front_body, half_lat),
        "front",
        [SCALARS] + [WHOLE] * 8 + [LEFT_OUT] + [WHOLE] * 4 + [LEFT_OUT] * len(after),
        [
            shaped((levels, rows, cols, width), BF16),
            shaped((coarse_tokens, 4 * width), BF16),
            shaped((coarse_tokens, coarse_width), BF16),
            shaped((coarse_tokens, coarse_width), BF16),
        ],
        [
            pltpu.VMEM((levels, ext_rows, cols + 16, width), F32),
            pltpu.VMEM((wins * tokens, width), F32),
            pltpu.VMEM((wins * tokens, 3 * width), BF16),
            pltpu.VMEM((wins * tokens, width), BF16),
            pltpu.VMEM((coarse_tokens, 4 * width), F32),
            pltpu.VMEM((coarse_tokens, 4 * width), BF16),
            pltpu.VMEM((levels, rows, width // LANES, cols, LANES), F32),
            pltpu.VMEM(merge_weight.shape, BF16),
            pltpu.SemaphoreType.DMA,
        ],
        30_000_000_000,
        12_000_000,
        flags, fine, top, bot, left, right, scale, qkv_weight, out_weight, merge_weight,
        mask, ones, lane, sums, *after,
        vmem=56 * MIB,
    )


def lay_blocks(place_ref, mid, last, near, far, dest):
    depth = dest.shape[0] // (DIMS[0] * DIMS[1] * DIMS[2])
    for stack, (mids, lasts) in enumerate((((0, 1), (0, 1, 3, 2)), ((3, 2), (0, 3, 1, 2)))):
        for at, k_last in enumerate(lasts):
            ref = near[stack] if at < 2 else far[stack]
            for m, k_mid in enumerate(mids):
                for k_first in range(DIMS[0]):
                    block = 0
                    for digit, k in ((0, k_first), (mid, k_mid), (last, k_last)):
                        block += jnp.bitwise_xor(place_ref[digit], k) * STRIDES[digit]
                    start = pl.multiple_of(block * depth, depth)
                    dest[pl.ds(start, depth), :] = ref[at % 2, m, k_first]


def prep_body(place_ref, *refs):
    up_parts, down_parts, cots = refs[:4], refs[4:8], refs[8:12]
    up_ref, up_t_ref, down_ref, near_ref, away_ref, down_t = refs[12:]
    lay_blocks(place_ref, 2, 1, up_parts[:2], up_parts[2:], up_ref)
    lay_blocks(place_ref, 1, 2, down_parts[:2], down_parts[2:], down_t)
    for j in range(4):
        n = cots[j].shape[0]
        grad_ref = near_ref if j < 2 else away_ref
        at = slice((j % 2) * n, (j % 2 + 1) * n)
        grad_ref[at, :] = dot_nn(cots[j][...], down_t[...]).astype(BF16)
    ff = up_ref.shape[1]
    step = 256
    for s in range(0, ff, step):
        up_t_ref[s : s + step, :] = up_ref[:, s : s + step].T
        down_ref[s : s + step, :] = down_t[:, s : s + step].T


def prep(place, up_parts, down_parts, cots):
    ff = up_parts[0].shape[-1]
    tokens, width = cots[0].shape
    return run_kernel(
        prep_body,
        "prep",
        [SCALARS] + [WHOLE] * 12,
        [
            shaped((width, ff), BF16),
            shaped((ff, width), BF16),
            shaped((ff, width), BF16),
            shaped((2 * tokens, ff), BF16),
            shaped((2 * tokens, ff), BF16),
        ],
        [pltpu.VMEM((width, ff), BF16)],
        8 * tokens * width * ff,
        12_000_000,
        place, *up_parts, *down_parts, *cots,
        vmem=56 * MIB,
    )


TERM_PARTS = (((0, 3), (0, 3)), ((1, 2), (0, 3)), ((0, 1), (1, 2)), ((3, 2), (1, 2)))


def term_into(held, place_ref, left, right, mid, last):
    width = left.shape[1]
    depth = held.shape[3]
    chunk = 256
    for s in range(0, width, chunk):
        total = dot_tn(left[:, s : s + chunk], right[...]).astype(BF16)
        for m in range(chunk // depth):
            block = s // depth + m
            k = [
                jnp.bitwise_xor(place_ref[digit], (block // STRIDES[digit]) % DIMS[digit])
                for digit in range(3)
            ]
            held[k[last], k[mid], k[0]] = total[m * depth : (m + 1) * depth, :]


def start_all(pairs, sems):
    copies = [pltpu.make_async_copy(a, b, sems.at[i]) for i, (a, b) in enumerate(pairs)]
    for copy in copies:
        copy.start()
    return copies


def activate(tokens, up, grads, hid, pre, rows):
    chunk = 256
    for s in range(0, up.shape[1], chunk):
        act = dot_nn(tokens, up[:, s : s + chunk])
        cdf = 0.5 + 0.5 * lax.erf(act * math.sqrt(0.5))
        hid[rows, s : s + chunk] = (act * cdf).astype(BF16)
        slope = cdf + act * (jnp.exp(-0.5 * (act * act)) * (1.0 / math.sqrt(2.0 * math.pi)))
        pre[rows, s : s + chunk] = (grads[rows, s : s + chunk].astype(F32) * slope).astype(BF16)


def near_body(first_ref, second_ref, grad_ref, up_ref, hid_ref, pre_ref):
    n = first_ref.shape[0]
    for j, tokens in enumerate((first_ref, second_ref)):
        activate(tokens[...], up_ref, grad_ref, hid_ref, pre_ref, slice(j * n, (j + 1) * n))


def feed_near(first, second, grads, up):
    n, width = first.shape
    ff = up.shape[1]
    return run_kernel(
        near_body,
        "feed_near",
        [WHOLE] * 4,
        [shaped((2 * n, ff), BF16)] * 2,
        [],
        0,
        0,
        first, second, grads, up,
        vmem=56 * MIB,
    )


def feed_body(place_ref, *refs):
    token_refs, cot_refs, refs = refs[:4], refs[4:8], refs[8:]
    (grad_hbm, hid_hbm, pre_hbm, up_hbm, up_t_hbm, down_hbm), refs = refs[:6], refs[6:]
    up_outs, down_outs, (near_hbm, away_hbm, send_hbm), refs = refs[:4], refs[4:8], refs[8:11], refs[11:]
    tok, cot, grads, up, up_t, down, hid, pre, held_u, held_d, near, away, send, ins, outs = refs
    n = token_refs[0].shape[0]
    first = pl.ds(0, 2 * n)
    pairs = [(up_hbm, up), (grad_hbm, grads)]
    pairs += [(token_refs[j], tok.at[pl.ds(j * n, n)]) for j in (2, 3)]
    pairs += [(hid_hbm, hid.at[first])]
    pairs += [(cot_refs[j], cot.at[pl.ds(j * n, n)]) for j in range(4)]
    pairs += [(token_refs[j], tok.at[pl.ds(j * n, n)]) for j in (0, 1)]
    pairs += [(pre_hbm, pre.at[first]), (up_t_hbm, up_t), (down_hbm, down)]
    fetches = start_all(pairs, ins)
    stores = []

    def store(src, dst):
        copy = pltpu.make_async_copy(src, dst, outs.at[len(stores)])
        copy.start()
        stores.append(copy)

    for k in range(4):
        fetches[k].wait()
    far = pl.ds(2 * n, 2 * n)
    for j in (2, 3):
        rows = slice((j - 2) * n, (j - 1) * n)
        activate(tok[j * n : (j + 1) * n, :], up, grads, hid.at[far], pre.at[far], rows)
    for k in range(4, 9):
        fetches[k].wait()
    for held, left, right, parts, mid, last in (
        (held_d, cot, hid, down_outs, 1, 2),
        (held_u, tok, pre, up_outs, 2, 1),
    ):
        if held is held_u:
            for k in range(9, 12):
                fetches[k].wait()
        term_into(held, place_ref, left, right, mid, last)
        for out, (lasts, mids) in zip(parts, TERM_PARTS):
            for i, k_last in enumerate(lasts):
                for m, k_mid in enumerate(mids):
                    store(held.at[k_last, k_mid], out.at[i, m])
    for which, (rows, weight) in enumerate(((pre, up_t), (hid, down))):
        fetches[12 + which].wait()
        for side, (keep, keep_hbm) in enumerate(((near, near_hbm), (away, away_hbm))):
            sums = dot_nn(rows[2 * side * n : 2 * (side + 1) * n, :], weight[...]).astype(BF16)
            keep[which] = sums[:n]
            send[2 * side + which] = sums[n:]
            store(keep.at[which], keep_hbm.at[which])
            store(send.at[2 * side + which], send_hbm.at[2 * side + which])
    for copy in stores:
        copy.wait()


def feed(place, tokens, cots, grads, near_hid, near_pre, up, up_t, down):
    n, width = tokens[0].shape
    ff = up.shape[1]
    depth = width // (DIMS[0] * DIMS[1] * DIMS[2])
    part = shaped((2, 2, DIMS[0], depth, ff), BF16)
    outs = [part] * 8 + [shaped((k, n, width), BF16) for k in (2, 2, 4)]
    result = pl.pallas_call(
        feed_body,
        name="feed",
        in_specs=[SCALARS] + [LEFT_OUT] * 14,
        out_specs=[LEFT_OUT] * len(outs),
        out_shape=outs,
        scratch_shapes=[
            pltpu.VMEM((4 * n, width), BF16),
            pltpu.VMEM((4 * n, width), BF16),
            pltpu.VMEM((2 * n, ff), BF16),
            pltpu.VMEM((width, ff), BF16),
            pltpu.VMEM((ff, width), BF16),
            pltpu.VMEM((ff, width), BF16),
            pltpu.VMEM((4 * n, ff), BF16),
            pltpu.VMEM((4 * n, ff), BF16),
            pltpu.VMEM((4, 4, DIMS[0], depth, ff), BF16),
            pltpu.VMEM((4, 4, DIMS[0], depth, ff), BF16),
            pltpu.VMEM((2, n, width), BF16),
            pltpu.VMEM((2, n, width), BF16),
            pltpu.VMEM((4, n, width), BF16),
            pltpu.SemaphoreType.DMA((14,)),
            pltpu.SemaphoreType.DMA((40,)),
        ],
        compiler_params=pltpu.CompilerParams(vmem_limit_bytes=56 * MIB),
        cost_estimate=pl.CostEstimate(flops=1000, bytes_accessed=1000, transcendentals=0),
    )(place, *tokens, *cots, grads, near_hid, near_pre, up, up_t, down)
    return result[:4], result[4:8], result[8:]


def last_body(coarse_ref, cot_ref, own_ref, there_ref, far_ref, cat_ref, merge_ref, *refs):
    skip_grad, slots, spread, shares, sems = refs[-5:]
    fetches = [
        pltpu.make_async_copy(ref.at[0], shares.at[k], sems.at[k])
        for k, ref in enumerate((own_ref, there_ref))
    ]
    for fetch in fetches:
        fetch.start()
    levels, rows, cols, width = skip_grad.shape
    coarse = coarse_ref[...].astype(F32)
    normed, inverse = centre_scale(coarse)
    for fetch in fetches:
        fetch.wait()
    grad = shares[0].astype(F32) + shares[1].astype(F32) + far_ref[...].astype(F32)
    back = inverse * (
        grad
        - jnp.mean(grad, -1, keepdims=True)
        - normed * jnp.mean(grad * normed, -1, keepdims=True)
    )
    coarse_grad = (cot_ref[...].astype(F32) + back).astype(BF16)
    slots[...] = dot_nt(coarse_grad, merge_ref[...])
    half = cols // 2
    step = 96
    for s in range(0, slots.shape[0], step):
        normed, inverse = centre_scale(cat_ref[s : s + step, :].astype(F32))
        grad = slots[s : s + step, :]
        slots[s : s + step, :] = inverse * (
            grad
            - jnp.mean(grad, -1, keepdims=True)
            - normed * jnp.mean(grad * normed, -1, keepdims=True)
        )
    for l in range(levels):
        for i in range(rows // 2):
            at = (l * (rows // 2) + i) * half
            for a in range(2):
                for b in range(2):
                    for q in range(width // LANES):
                        to = (a + 2 * b) * width + q * LANES
                        spread[l, 2 * i + a, q, pl.ds(b, half, 2), :] = slots[
                            at : at + half, to : to + LANES
                        ]

    def lay_out(row, carry):
        for l in range(levels):
            for q in range(width // LANES):
                skip_grad[l, row, :, q * LANES : (q + 1) * LANES] = spread[l, row, q]
        return carry

    lax.fori_loop(0, rows, lay_out, 0)


def last(coarse, cot, own, there, far, cat, merge_weight, fine_shape, after):
    levels, rows, cols, width = fine_shape
    return run_kernel(
        last_body,
        "last",
        [WHOLE] * 2 + [LEFT_OUT] * 2 + [WHOLE] * 3 + [LEFT_OUT] * len(after),
        [shaped(fine_shape, F32)],
        [
            pltpu.VMEM(cat.shape, F32),
            pltpu.VMEM((levels, rows, width // LANES, cols, LANES), F32),
            pltpu.VMEM((2, *own.shape[1:]), BF16),
            pltpu.SemaphoreType.DMA((2,)),
        ],
        2 * cat.shape[0] * merge_weight.shape[0] * merge_weight.shape[1],
        10_000_000,
        coarse, cot, own, there, far, cat, merge_weight, *after,
        vmem=30 * MIB,
    )[0]


def with_rows(cells, width):
    count = lax.axis_size("lat")
    above = lax.ppermute(
        cells[:, -width:], "lat", [(i, (i + 1) % count) for i in range(count)]
    )
    below = lax.ppermute(cells[:, :width], "lat", [((i + 1) % count, i) for i in range(count)])
    return above, below


def on_device(
    fine_field, head_scale, qkv_weight, out_weight, merge_weight, up_weight, down_weight, cotangent
):
    levels, lat_rows, lon_cols, channels = fine_field.shape
    coarse_width = merge_weight.shape[1]
    half_lat, half_lon = WH // 2, WW // 2
    lon_count = lax.axis_size("lon")
    me = lax.axis_index("lon")
    place = jnp.stack([(me // STRIDES[d]) % DIMS[d] for d in range(3)]).astype(jnp.int32)

    weights = jnp.stack([up_weight, down_weight.T])[:, None]
    weights = jnp.concatenate([weights, lon_swap(weights, 0, 1)], 1)
    top, bot = with_rows(fine_field, half_lat)
    tall = [
        jnp.concatenate([top[:, :, cut], fine_field[:, :, cut], bot[:, :, cut]], 1)
        for cut in (slice(lon_cols - half_lon, lon_cols), slice(0, half_lon))
    ]
    left = lax.ppermute(tall[0], "lon", [(i, (i + 1) % lon_count) for i in range(lon_count)])
    right = lax.ppermute(tall[1], "lon", [((i + 1) % lon_count, i) for i in range(lon_count)])
    up_near = gather_near(gather_mid(weights[0], 2), 1)
    down_near = gather_near(gather_mid(weights[1], 1), 2)
    cot = cotangent.reshape(-1, coarse_width)
    held, _, _ = lax.optimization_barrier((cot, left, right))
    cot_c, cot_y = lat_swap(held, 1), lat_swap(held, 2)
    skip_field, cat, coarse, normed = front(
        fine_field, top, bot, left, right, head_scale, qkv_weight, out_weight, merge_weight,
        (*up_near, *down_near, cot_c),
    )
    up_far, down_far = gather_far(up_near, 1), gather_far(down_near, 2)
    normed, up_far, down_far, cot_y = lax.optimization_barrier((normed, up_far, down_far, cot_y))
    cots = [cot, cot_c, cot_y, lat_swap(cot_y, 1)]
    normed_c, normed_y = lat_swap(normed, 1), lat_swap(normed, 2)
    up, up_t, down, near_grad, away_grad = prep(
        place, (*up_near, *up_far), (*down_near, *down_far), cots
    )
    near_hid, near_pre = feed_near(normed, normed_c, near_grad, up)
    normed_y, near_hid = lax.optimization_barrier((normed_y, near_hid))
    tokens = [normed, normed_c, normed_y, lat_swap(normed_y, 1)]

    def scatter_one(parts, digit):
        return lon_swap(parts[1], digit, 1), lon_swap(parts[3], digit, 3)

    def scatter_two(parts, came, digit):
        keep = [add_parts(parts[2 * h][0], came[h][0]) for h in range(2)]
        send = [add_parts(parts[2 * h][1], came[h][1]) for h in range(2)]
        return keep, send, (lon_swap(send[0], digit, 3), lon_swap(send[1], digit, 1))

    term_up, term_down, (near, away, send) = feed(
        place, tokens, cots, away_grad, near_hid, near_pre, up, up_t, down
    )
    there = lat_swap(send, 1)
    up_came, down_came = scatter_one(term_up, 1), scatter_one(term_down, 2)
    back_pass = add_parts(away[0], there[2])
    back_far = lat_swap(back_pass, 2)
    up_came, down_came, back_pass = lax.optimization_barrier((up_came, down_came, back_pass))
    up_keep, _, up_came = scatter_two(term_up, up_came, 1)
    down_keep, _, down_came = scatter_two(term_down, down_came, 2)
    up_halves = [add_parts(up_keep[h], up_came[h]) for h in range(2)]
    down_halves = [add_parts(down_keep[h], down_came[h]) for h in range(2)]
    up_came, down_came = lon_swap(up_halves[1], 2, 1), lon_swap(down_halves[1], 1, 1)
    out_pass = add_parts(away[1], there[3])
    out_far = lat_swap(out_pass, 2)
    skip_grad = last(
        coarse, cot, near, there, back_far, cat, merge_weight, fine_field.shape,
        (up_halves[1], down_halves[1]),
    )
    up_came, down_came, skip_grad = lax.optimization_barrier((up_came, down_came, skip_grad))
    up_pair, down_pair = add_parts(up_halves[0], up_came), add_parts(down_halves[0], down_came)
    up_end = add_parts(up_pair[0], lon_swap(up_pair[1], 2, 3))
    down_end = add_parts(down_pair[0], lon_swap(down_pair[1], 1, 3))
    both = jnp.stack([up_end, down_end], 1)
    both = both[0].astype(F32) + lon_swap(both[1], 0, 1).astype(F32)
    coarse_out = (
        coarse.astype(F32)
        + (near[1].astype(F32) + there[1].astype(F32) + out_far.astype(F32))
    ).astype(BF16)
    return (
        skip_field,
        coarse_out.reshape(levels, lat_rows // 2, lon_cols // 2, coarse_width),
        both[0],
        both[1].T,
        skip_grad,
    )


def solution(mesh):
    placed = (
        P(None, "lat", "lon", None),
        P(),
        P(),
        P(),
        P(),
        P("lon", "lat"),
        P("lat", "lon"),
        P(None, "lat", "lon", None),
    )
    return jax.shard_map(
        on_device,
        mesh=mesh,
        in_specs=placed,
        out_specs=(
            P(None, "lat", "lon", None),
            P(None, "lat", "lon", None),
            P("lon", "lat"),
            P("lat", "lon"),
            P(None, "lat", "lon", None),
        ),
        check_vma=False,
    )
```

```python
import functools
import math

import jax
import jax.numpy as jnp
import numpy as np
from jax import lax
from jax.experimental import pallas as pl
from jax.experimental.pallas import tpu as pltpu
from jax.sharding import PartitionSpec as P

WH = 6
WW = 12
HEAD = 32
LANES = 128
GROUP = 4
F32 = jnp.float32
BF16 = jnp.bfloat16
MIB = 1024 * 1024

WHOLE = pl.BlockSpec(memory_space=pltpu.VMEM)
SCALARS = pl.BlockSpec(memory_space=pltpu.SMEM)
LEFT_OUT = pl.BlockSpec(memory_space=pl.ANY)


def run_kernel(body, name, specs, outs, scratch, flops, moved, *operands, vmem):
    return pl.pallas_call(
        body,
        name=name,
        in_specs=specs,
        out_specs=[WHOLE] * len(outs),
        out_shape=outs,
        scratch_shapes=scratch,
        compiler_params=pltpu.CompilerParams(vmem_limit_bytes=vmem),
        cost_estimate=pl.CostEstimate(flops=1000, bytes_accessed=1000, transcendentals=0),
    )(*operands)


def shaped(shape, kind):
    return jax.ShapeDtypeStruct(shape, kind)


def dot_nn(left, right):
    return lax.dot_general(left, right, (((1,), (0,)), ((), ())), preferred_element_type=F32)


def dot_nt(left, right):
    return lax.dot_general(left, right, (((1,), (1,)), ((), ())), preferred_element_type=F32)


def dot_tn(left, right):
    return lax.dot_general(left, right, (((0,), (0,)), ((), ())), preferred_element_type=F32)


def centre_scale(rows):
    centred = rows - jnp.mean(rows, -1, keepdims=True)
    inverse = lax.rsqrt(jnp.mean(centred * centred, -1, keepdims=True) + 1e-05)
    return centred * inverse, inverse


DIMS = (2, 4, 4)
STRIDES = (16, 4, 1)


def lat_swap(array, bits):
    count = lax.axis_size("lat")
    return lax.ppermute(array, "lat", [(i, i ^ bits) for i in range(count)])


def lon_swap(array, digit, bits):
    count = lax.axis_size("lon")
    return lax.ppermute(array, "lon", [(i, i ^ (bits * STRIDES[digit])) for i in range(count)])


def add_parts(*arrays):
    return sum(array.astype(F32) for array in arrays).astype(BF16)


def gather_mid(own, digit):
    pair = jnp.stack([own, lon_swap(own, digit, 1)])
    return pair, lon_swap(pair, digit, 3)


def gather_near(stacks, digit):
    first, second = stacks
    return (
        jnp.stack([first, lon_swap(first, digit, 1)]),
        jnp.stack([second, lon_swap(second, digit, 3)]),
    )


def gather_far(near, digit):
    return lon_swap(near[0], digit, 3), lon_swap(near[1], digit, 1)


def front_body(
    half_lat, flag_ref, x_ref, top_ref, bot_ref, left_ref, right_ref, scale_ref, qkv_w, out_w,
    merge_hbm, mask_ref, ones_ref, lane_ref, sums_ref, *refs,
):
    (
        skip_ref, cat_ref, coarse_ref, normed_ref,
        ext, xw, qkv, att, cat, catn, spread, merge_w, sem,
    ) = refs[-13:]
    levels, rows, cols, width = x_ref.shape
    fetch = pltpu.make_async_copy(merge_hbm, merge_w, sem)
    fetch.start()
    lead = 8
    half_lon = left_ref.shape[2]
    tokens = levels * WH * WW
    wins = (cols + 2 * half_lon) // WW

    def fill(row, carry):
        for l in range(levels):
            ext[l, half_lat + row, lead : lead + cols, :] = x_ref[l, row].astype(F32)
        return carry

    lax.fori_loop(0, rows, fill, 0)
    for l in range(levels):
        for r in range(half_lat):
            ext[l, r, lead : lead + cols, :] = top_ref[l, r].astype(F32)
            ext[l, half_lat + rows + r, lead : lead + cols, :] = bot_ref[l, r].astype(F32)

    def fill_sides(row, carry):
        for l in range(levels):
            ext[l, row, lead - half_lon : lead, :] = left_ref[l, row].astype(F32)
            ext[l, row, lead + cols : lead + cols + half_lon, :] = right_ref[l, row].astype(F32)
        return carry

    lax.fori_loop(0, rows + 2 * half_lat, fill_sides, 0)

    chunk = 256
    sections = width // chunk
    groups = width // (GROUP * HEAD)
    lanes = GROUP * HEAD

    def places():
        for c in range(wins):
            for l in range(levels):
                for r in range(WH):
                    yield c, l, r

    def band(b, carry):
        for c, l, r in places():
            at = c * tokens + (l * WH + r) * WW
            start = lead - half_lon + c * WW
            xw[at : at + WW, :] = ext[l, b * WH + r, start : start + WW, :]
        normed = centre_scale(xw[...])[0].astype(BF16)
        for j in range(3 * sections):
            y = dot_nn(normed, qkv_w[:, j * chunk : (j + 1) * chunk])
            if j < 2 * sections:
                square = y * y
                high = square.astype(BF16)
                low = (square - high.astype(F32)).astype(BF16)
                total = dot_nn(high, ones_ref[...]) + dot_nn(low, ones_ref[...])
                y = y * lax.rsqrt(total + 1e-06)
                if j < sections:
                    y = y * scale_ref[:, j * chunk : (j + 1) * chunk]
            qkv[:, j * chunk : (j + 1) * chunk] = y.astype(BF16)
        allowed = mask_ref[flag_ref[b]]
        for c in range(wins):
            rows_at = slice(c * tokens, (c + 1) * tokens)
            for g in range(groups):
                q = qkv[rows_at, g * lanes : (g + 1) * lanes]
                k = qkv[rows_at, width + g * lanes : width + (g + 1) * lanes]
                v = qkv[rows_at, 2 * width + g * lanes : 2 * width + (g + 1) * lanes]
                k4 = jnp.concatenate([k * lane_ref[h : h + 1, :] for h in range(GROUP)], 0)
                v4 = jnp.concatenate([v * lane_ref[h : h + 1, :] for h in range(GROUP)], 0)
                weight = jnp.exp2(dot_nt(q, k4)).astype(BF16) * allowed
                both = dot_nn(weight, jnp.concatenate([v4, sums_ref[...]], 1))
                att[rows_at, g * lanes : (g + 1) * lanes] = (
                    both[:, :lanes] / both[:, lanes:]
                ).astype(BF16)
        skip = xw[...] + dot_nn(att[...], out_w[...])
        xw[...] = skip.astype(BF16).astype(F32)
        for c, l, r in places():
            at = c * tokens + (l * WH + r) * WW
            start = lead - half_lon + c * WW
            ext[l, b * WH + r, start : start + WW, :] = xw[at : at + WW, :]
        return carry

    lax.fori_loop(0, (rows + 2 * half_lat) // WH, band, 0)

    def store_skip(row, carry):
        for l in range(levels):
            line = ext[l, half_lat + row, lead : lead + cols, :]
            skip_ref[l, row] = line.astype(BF16)
            for q in range(width // LANES):
                spread[l, row, q] = line[:, q * LANES : (q + 1) * LANES]
        return carry

    lax.fori_loop(0, rows, store_skip, 0)
    half = cols // 2
    for l in range(levels):
        for i in range(rows // 2):
            at = (l * (rows // 2) + i) * half
            for a in range(2):
                for b in range(2):
                    for q in range(width // LANES):
                        to = (a + 2 * b) * width + q * LANES
                        cat[at : at + half, to : to + LANES] = spread[
                            l, 2 * i + a, q, pl.ds(b, half, 2), :
                        ]
    total = cat.shape[0]
    step = 96
    for s in range(0, total, step):
        piece = cat[s : s + step, :]
        cat_ref[s : s + step, :] = piece.astype(BF16)
        catn[s : s + step, :] = centre_scale(piece)[0].astype(BF16)
    fetch.wait()
    coarse = dot_nn(catn[...], merge_w[...]).astype(BF16)
    coarse_ref[...] = coarse
    normed_ref[...] = centre_scale(coarse.astype(F32))[0].astype(BF16)


def front(fine, top, bot, left, right, head_scale, qkv_weight, out_weight, merge_weight, after):
    levels, rows, cols, width = fine.shape
    half_lat = WH // 2
    tokens = levels * WH * WW
    ext_rows = rows + 2 * half_lat
    bands = ext_rows // WH
    wins = (cols + WW) // WW
    heads = head_scale.shape[0]
    coarse_width = merge_weight.shape[1]
    coarse_tokens = levels * rows * cols // 4
    lat_place = lax.axis_index("lat")
    lat_last = lax.axis_size("lat") - 1
    band_ids = jnp.arange(bands)
    flags = (
        ((band_ids == 0) & (lat_place == 0)) | ((band_ids == bands - 1) & (lat_place == lat_last))
    ).astype(jnp.int32)
    scale = jnp.repeat(head_scale * (1.0 / math.log(2.0)), width // heads).reshape(1, width)
    group = (np.arange(tokens) // WW) % WH < half_lat
    same = np.tile(group[:, None] == group[None, :], (1, GROUP))
    mask = jnp.asarray(np.stack([np.ones_like(same), same]), BF16)
    lane_head = np.arange(256) // HEAD
    ones = jnp.asarray(lane_head[:, None] == lane_head[None, :], BF16)
    lane = jnp.asarray(np.arange(GROUP)[:, None] == lane_head[None, : GROUP * HEAD], BF16)
    sums = jnp.asarray(
        np.repeat(np.arange(GROUP), tokens)[:, None] == lane_head[None, : GROUP * HEAD], BF16
    )
    return run_kernel(
        functools.partial(front_body, half_lat),
        "front",
        [SCALARS] + [WHOLE] * 8 + [LEFT_OUT] + [WHOLE] * 4 + [LEFT_OUT] * len(after),
        [
            shaped((levels, rows, cols, width), BF16),
            shaped((coarse_tokens, 4 * width), BF16),
            shaped((coarse_tokens, coarse_width), BF16),
            shaped((coarse_tokens, coarse_width), BF16),
        ],
        [
            pltpu.VMEM((levels, ext_rows, cols + 16, width), F32),
            pltpu.VMEM((wins * tokens, width), F32),
            pltpu.VMEM((wins * tokens, 3 * width), BF16),
            pltpu.VMEM((wins * tokens, width), BF16),
            pltpu.VMEM((coarse_tokens, 4 * width), F32),
            pltpu.VMEM((coarse_tokens, 4 * width), BF16),
            pltpu.VMEM((levels, rows, width // LANES, cols, LANES), F32),
            pltpu.VMEM(merge_weight.shape, BF16),
            pltpu.SemaphoreType.DMA,
        ],
        30_000_000_000,
        12_000_000,
        flags, fine, top, bot, left, right, scale, qkv_weight, out_weight, merge_weight,
        mask, ones, lane, sums, *after,
        vmem=56 * MIB,
    )


def lay_blocks(place_ref, mid, last, near, far, dest):
    depth = dest.shape[0] // (DIMS[0] * DIMS[1] * DIMS[2])
    for stack, (mids, lasts) in enumerate((((0, 1), (0, 1, 3, 2)), ((3, 2), (0, 3, 1, 2)))):
        for at, k_last in enumerate(lasts):
            ref = near[stack] if at < 2 else far[stack]
            for m, k_mid in enumerate(mids):
                for k_first in range(DIMS[0]):
                    block = 0
                    for digit, k in ((0, k_first), (mid, k_mid), (last, k_last)):
                        block += jnp.bitwise_xor(place_ref[digit], k) * STRIDES[digit]
                    start = pl.multiple_of(block * depth, depth)
                    dest[pl.ds(start, depth), :] = ref[at % 2, m, k_first]


def prep_body(place_ref, *refs):
    up_parts, down_parts, cots = refs[:4], refs[4:8], refs[8:12]
    up_ref, up_t_ref, down_ref, near_ref, away_ref, down_t = refs[12:]
    lay_blocks(place_ref, 2, 1, up_parts[:2], up_parts[2:], up_ref)
    lay_blocks(place_ref, 1, 2, down_parts[:2], down_parts[2:], down_t)
    for j in range(4):
        n = cots[j].shape[0]
        grad_ref = near_ref if j < 2 else away_ref
        at = slice((j % 2) * n, (j % 2 + 1) * n)
        grad_ref[at, :] = dot_nn(cots[j][...], down_t[...]).astype(BF16)
    ff = up_ref.shape[1]
    step = 256
    for s in range(0, ff, step):
        up_t_ref[s : s + step, :] = up_ref[:, s : s + step].T
        down_ref[s : s + step, :] = down_t[:, s : s + step].T


def prep(place, up_parts, down_parts, cots):
    ff = up_parts[0].shape[-1]
    tokens, width = cots[0].shape
    return run_kernel(
        prep_body,
        "prep",
        [SCALARS] + [WHOLE] * 12,
        [
            shaped((width, ff), BF16),
            shaped((ff, width), BF16),
            shaped((ff, width), BF16),
            shaped((2 * tokens, ff), BF16),
            shaped((2 * tokens, ff), BF16),
        ],
        [pltpu.VMEM((width, ff), BF16)],
        8 * tokens * width * ff,
        12_000_000,
        place, *up_parts, *down_parts, *cots,
        vmem=56 * MIB,
    )


TERM_PARTS = (((0, 3), (0, 3)), ((1, 2), (0, 3)), ((0, 1), (1, 2)), ((3, 2), (1, 2)))


def term_into(held, place_ref, left, right, mid, last):
    width = left.shape[1]
    depth = held.shape[3]
    chunk = 256
    for s in range(0, width, chunk):
        total = dot_tn(left[:, s : s + chunk], right[...]).astype(BF16)
        for m in range(chunk // depth):
            block = s // depth + m
            k = [
                jnp.bitwise_xor(place_ref[digit], (block // STRIDES[digit]) % DIMS[digit])
                for digit in range(3)
            ]
            held[k[last], k[mid], k[0]] = total[m * depth : (m + 1) * depth, :]


def start_all(pairs, sems):
    copies = [pltpu.make_async_copy(a, b, sems.at[i]) for i, (a, b) in enumerate(pairs)]
    for copy in copies:
        copy.start()
    return copies


def activate(tokens, up, grads, hid, pre, rows):
    chunk = 256
    for s in range(0, up.shape[1], chunk):
        act = dot_nn(tokens, up[:, s : s + chunk])
        cdf = 0.5 + 0.5 * lax.erf(act * math.sqrt(0.5))
        hid[rows, s : s + chunk] = (act * cdf).astype(BF16)
        slope = cdf + act * (jnp.exp(-0.5 * (act * act)) * (1.0 / math.sqrt(2.0 * math.pi)))
        pre[rows, s : s + chunk] = (grads[rows, s : s + chunk].astype(F32) * slope).astype(BF16)


def near_body(first_ref, second_ref, grad_ref, up_ref, hid_ref, pre_ref):
    n = first_ref.shape[0]
    for j, tokens in enumerate((first_ref, second_ref)):
        activate(tokens[...], up_ref, grad_ref, hid_ref, pre_ref, slice(j * n, (j + 1) * n))


def feed_near(first, second, grads, up):
    n, width = first.shape
    ff = up.shape[1]
    return run_kernel(
        near_body,
        "feed_near",
        [WHOLE] * 4,
        [shaped((2 * n, ff), BF16)] * 2,
        [],
        0,
        0,
        first, second, grads, up,
        vmem=56 * MIB,
    )


def feed_body(place_ref, *refs):
    token_refs, cot_refs, refs = refs[:4], refs[4:8], refs[8:]
    (grad_hbm, hid_hbm, pre_hbm, up_hbm, up_t_hbm, down_hbm), refs = refs[:6], refs[6:]
    up_outs, down_outs, (near_hbm, away_hbm, send_hbm), refs = refs[:4], refs[4:8], refs[8:11], refs[11:]
    tok, cot, grads, up, up_t, down, hid, pre, held_u, held_d, near, away, send, ins, outs = refs
    n = token_refs[0].shape[0]
    first = pl.ds(0, 2 * n)
    pairs = [(up_hbm, up), (grad_hbm, grads)]
    pairs += [(token_refs[j], tok.at[pl.ds(j * n, n)]) for j in (2, 3)]
    pairs += [(hid_hbm, hid.at[first])]
    pairs += [(cot_refs[j], cot.at[pl.ds(j * n, n)]) for j in range(4)]
    pairs += [(token_refs[j], tok.at[pl.ds(j * n, n)]) for j in (0, 1)]
    pairs += [(pre_hbm, pre.at[first]), (up_t_hbm, up_t), (down_hbm, down)]
    fetches = start_all(pairs, ins)
    stores = []

    def store(src, dst):
        copy = pltpu.make_async_copy(src, dst, outs.at[len(stores)])
        copy.start()
        stores.append(copy)

    for k in range(4):
        fetches[k].wait()
    far = pl.ds(2 * n, 2 * n)
    for j in (2, 3):
        rows = slice((j - 2) * n, (j - 1) * n)
        activate(tok[j * n : (j + 1) * n, :], up, grads, hid.at[far], pre.at[far], rows)
    for k in range(4, 9):
        fetches[k].wait()
    for held, left, right, parts, mid, last in (
        (held_d, cot, hid, down_outs, 1, 2),
        (held_u, tok, pre, up_outs, 2, 1),
    ):
        if held is held_u:
            for k in range(9, 12):
                fetches[k].wait()
        term_into(held, place_ref, left, right, mid, last)
        for out, (lasts, mids) in zip(parts, TERM_PARTS):
            for i, k_last in enumerate(lasts):
                for m, k_mid in enumerate(mids):
                    store(held.at[k_last, k_mid], out.at[i, m])
    for which, (rows, weight) in enumerate(((pre, up_t), (hid, down))):
        fetches[12 + which].wait()
        for side, (keep, keep_hbm) in enumerate(((near, near_hbm), (away, away_hbm))):
            sums = dot_nn(rows[2 * side * n : 2 * (side + 1) * n, :], weight[...]).astype(BF16)
            keep[which] = sums[:n]
            send[2 * side + which] = sums[n:]
            store(keep.at[which], keep_hbm.at[which])
            store(send.at[2 * side + which], send_hbm.at[2 * side + which])
    for copy in stores:
        copy.wait()


def feed(place, tokens, cots, grads, near_hid, near_pre, up, up_t, down):
    n, width = tokens[0].shape
    ff = up.shape[1]
    depth = width // (DIMS[0] * DIMS[1] * DIMS[2])
    part = shaped((2, 2, DIMS[0], depth, ff), BF16)
    outs = [part] * 8 + [shaped((k, n, width), BF16) for k in (2, 2, 4)]
    result = pl.pallas_call(
        feed_body,
        name="feed",
        in_specs=[SCALARS] + [LEFT_OUT] * 14,
        out_specs=[LEFT_OUT] * len(outs),
        out_shape=outs,
        scratch_shapes=[
            pltpu.VMEM((4 * n, width), BF16),
            pltpu.VMEM((4 * n, width), BF16),
            pltpu.VMEM((2 * n, ff), BF16),
            pltpu.VMEM((width, ff), BF16),
            pltpu.VMEM((ff, width), BF16),
            pltpu.VMEM((ff, width), BF16),
            pltpu.VMEM((4 * n, ff), BF16),
            pltpu.VMEM((4 * n, ff), BF16),
            pltpu.VMEM((4, 4, DIMS[0], depth, ff), BF16),
            pltpu.VMEM((4, 4, DIMS[0], depth, ff), BF16),
            pltpu.VMEM((2, n, width), BF16),
            pltpu.VMEM((2, n, width), BF16),
            pltpu.VMEM((4, n, width), BF16),
            pltpu.SemaphoreType.DMA((14,)),
            pltpu.SemaphoreType.DMA((40,)),
        ],
        compiler_params=pltpu.CompilerParams(vmem_limit_bytes=56 * MIB),
        cost_estimate=pl.CostEstimate(flops=1000, bytes_accessed=1000, transcendentals=0),
    )(place, *tokens, *cots, grads, near_hid, near_pre, up, up_t, down)
    return result[:4], result[4:8], result[8:]


def last_body(coarse_ref, cot_ref, own_ref, there_ref, far_ref, cat_ref, merge_ref, *refs):
    skip_grad, slots, spread, shares, sems = refs[-5:]
    fetches = [
        pltpu.make_async_copy(ref.at[0], shares.at[k], sems.at[k])
        for k, ref in enumerate((own_ref, there_ref))
    ]
    for fetch in fetches:
        fetch.start()
    levels, rows, cols, width = skip_grad.shape
    coarse = coarse_ref[...].astype(F32)
    normed, inverse = centre_scale(coarse)
    for fetch in fetches:
        fetch.wait()
    grad = shares[0].astype(F32) + shares[1].astype(F32) + far_ref[...].astype(F32)
    back = inverse * (
        grad
        - jnp.mean(grad, -1, keepdims=True)
        - normed * jnp.mean(grad * normed, -1, keepdims=True)
    )
    coarse_grad = (cot_ref[...].astype(F32) + back).astype(BF16)
    slots[...] = dot_nt(coarse_grad, merge_ref[...])
    half = cols // 2
    step = 96
    for s in range(0, slots.shape[0], step):
        normed, inverse = centre_scale(cat_ref[s : s + step, :].astype(F32))
        grad = slots[s : s + step, :]
        slots[s : s + step, :] = inverse * (
            grad
            - jnp.mean(grad, -1, keepdims=True)
            - normed * jnp.mean(grad * normed, -1, keepdims=True)
        )
    for l in range(levels):
        for i in range(rows // 2):
            at = (l * (rows // 2) + i) * half
            for a in range(2):
                for b in range(2):
                    for q in range(width // LANES):
                        to = (a + 2 * b) * width + q * LANES
                        spread[l, 2 * i + a, q, pl.ds(b, half, 2), :] = slots[
                            at : at + half, to : to + LANES
                        ]

    def lay_out(row, carry):
        for l in range(levels):
            for q in range(width // LANES):
                skip_grad[l, row, :, q * LANES : (q + 1) * LANES] = spread[l, row, q]
        return carry

    lax.fori_loop(0, rows, lay_out, 0)


def last(coarse, cot, own, there, far, cat, merge_weight, fine_shape, after):
    levels, rows, cols, width = fine_shape
    return run_kernel(
        last_body,
        "last",
        [WHOLE] * 2 + [LEFT_OUT] * 2 + [WHOLE] * 3 + [LEFT_OUT] * len(after),
        [shaped(fine_shape, F32)],
        [
            pltpu.VMEM(cat.shape, F32),
            pltpu.VMEM((levels, rows, width // LANES, cols, LANES), F32),
            pltpu.VMEM((2, *own.shape[1:]), BF16),
            pltpu.SemaphoreType.DMA((2,)),
        ],
        2 * cat.shape[0] * merge_weight.shape[0] * merge_weight.shape[1],
        10_000_000,
        coarse, cot, own, there, far, cat, merge_weight, *after,
        vmem=30 * MIB,
    )[0]


def with_rows(cells, width):
    count = lax.axis_size("lat")
    above = lax.ppermute(
        cells[:, -width:], "lat", [(i, (i + 1) % count) for i in range(count)]
    )
    below = lax.ppermute(cells[:, :width], "lat", [((i + 1) % count, i) for i in range(count)])
    return above, below


def on_device(
    fine_field, head_scale, qkv_weight, out_weight, merge_weight, up_weight, down_weight, cotangent
):
    levels, lat_rows, lon_cols, channels = fine_field.shape
    coarse_width = merge_weight.shape[1]
    half_lat, half_lon = WH // 2, WW // 2
    lon_count = lax.axis_size("lon")
    me = lax.axis_index("lon")
    place = jnp.stack([(me // STRIDES[d]) % DIMS[d] for d in range(3)]).astype(jnp.int32)

    weights = jnp.stack([up_weight, down_weight.T])[:, None]
    weights = jnp.concatenate([weights, lon_swap(weights, 0, 1)], 1)
    top, bot = with_rows(fine_field, half_lat)
    tall = [
        jnp.concatenate([top[:, :, cut], fine_field[:, :, cut], bot[:, :, cut]], 1)
        for cut in (slice(lon_cols - half_lon, lon_cols), slice(0, half_lon))
    ]
    left = lax.ppermute(tall[0], "lon", [(i, (i + 1) % lon_count) for i in range(lon_count)])
    right = lax.ppermute(tall[1], "lon", [((i + 1) % lon_count, i) for i in range(lon_count)])
    up_near = gather_near(gather_mid(weights[0], 2), 1)
    down_near = gather_near(gather_mid(weights[1], 1), 2)
    cot = cotangent.reshape(-1, coarse_width)
    held, _, _ = lax.optimization_barrier((cot, left, right))
    cot_c, cot_y = lat_swap(held, 1), lat_swap(held, 2)
    skip_field, cat, coarse, normed = front(
        fine_field, top, bot, left, right, head_scale, qkv_weight, out_weight, merge_weight,
        (*up_near, *down_near, cot_c),
    )
    up_far, down_far = gather_far(up_near, 1), gather_far(down_near, 2)
    normed, up_far, down_far, cot_y = lax.optimization_barrier((normed, up_far, down_far, cot_y))
    cots = [cot, cot_c, cot_y, lat_swap(cot_y, 1)]
    normed_c, normed_y = lat_swap(normed, 1), lat_swap(normed, 2)
    up, up_t, down, near_grad, away_grad = prep(
        place, (*up_near, *up_far), (*down_near, *down_far), cots
    )
    near_hid, near_pre = feed_near(normed, normed_c, near_grad, up)
    normed_y, near_hid = lax.optimization_barrier((normed_y, near_hid))
    tokens = [normed, normed_c, normed_y, lat_swap(normed_y, 1)]

    def scatter_one(parts, digit):
        return lon_swap(parts[1], digit, 1), lon_swap(parts[3], digit, 3)

    def scatter_two(parts, came, digit):
        keep = [add_parts(parts[2 * h][0], came[h][0]) for h in range(2)]
        send = [add_parts(parts[2 * h][1], came[h][1]) for h in range(2)]
        return keep, send, (lon_swap(send[0], digit, 3), lon_swap(send[1], digit, 1))

    term_up, term_down, (near, away, send) = feed(
        place, tokens, cots, away_grad, near_hid, near_pre, up, up_t, down
    )
    there = lat_swap(send, 1)
    up_came, down_came = scatter_one(term_up, 1), scatter_one(term_down, 2)
    back_pass = add_parts(away[0], there[2])
    back_far = lat_swap(back_pass, 2)
    up_came, down_came, back_pass = lax.optimization_barrier((up_came, down_came, back_pass))
    up_keep, _, up_came = scatter_two(term_up, up_came, 1)
    down_keep, _, down_came = scatter_two(term_down, down_came, 2)
    up_halves = [add_parts(up_keep[h], up_came[h]) for h in range(2)]
    down_halves = [add_parts(down_keep[h], down_came[h]) for h in range(2)]
    up_came, down_came = lon_swap(up_halves[1], 2, 1), lon_swap(down_halves[1], 1, 1)
    out_pass = add_parts(away[1], there[3])
    out_far = lat_swap(out_pass, 2)
    held, up_halves, down_halves = lax.optimization_barrier((coarse, up_halves, down_halves))
    skip_grad = last(held, cot, near, there, back_far, cat, merge_weight, fine_field.shape, ())
    up_came, down_came, skip_grad = lax.optimization_barrier((up_came, down_came, skip_grad))
    up_pair, down_pair = add_parts(up_halves[0], up_came), add_parts(down_halves[0], down_came)
    up_end = add_parts(up_pair[0], lon_swap(up_pair[1], 2, 3))
    down_end = add_parts(down_pair[0], lon_swap(down_pair[1], 1, 3))
    both = jnp.stack([up_end, down_end], 1)
    both = both[0].astype(F32) + lon_swap(both[1], 0, 1).astype(F32)
    coarse_out = (
        coarse.astype(F32)
        + (near[1].astype(F32) + there[1].astype(F32) + out_far.astype(F32))
    ).astype(BF16)
    return (
        skip_field,
        coarse_out.reshape(levels, lat_rows // 2, lon_cols // 2, coarse_width),
        both[0],
        both[1].T,
        skip_grad,
    )


def solution(mesh):
    placed = (
        P(None, "lat", "lon", None),
        P(),
        P(),
        P(),
        P(),
        P("lon", "lat"),
        P("lat", "lon"),
        P(None, "lat", "lon", None),
    )
    return jax.shard_map(
        on_device,
        mesh=mesh,
        in_specs=placed,
        out_specs=(
            P(None, "lat", "lon", None),
            P(None, "lat", "lon", None),
            P("lon", "lat"),
            P("lat", "lon"),
            P(None, "lat", "lon", None),
        ),
        check_vma=False,
    )
```

```python
import functools
import math

import jax
import jax.numpy as jnp
import numpy as np
from jax import lax
from jax.experimental import pallas as pl
from jax.experimental.pallas import tpu as pltpu
from jax.sharding import PartitionSpec as P

WH = 6
WW = 12
HEAD = 32
LANES = 128
GROUP = 4
F32 = jnp.float32
BF16 = jnp.bfloat16
MIB = 1024 * 1024

WHOLE = pl.BlockSpec(memory_space=pltpu.VMEM)
SCALARS = pl.BlockSpec(memory_space=pltpu.SMEM)
LEFT_OUT = pl.BlockSpec(memory_space=pl.ANY)


def run_kernel(body, name, specs, outs, scratch, flops, moved, *operands, vmem):
    return pl.pallas_call(
        body,
        name=name,
        in_specs=specs,
        out_specs=[WHOLE] * len(outs),
        out_shape=outs,
        scratch_shapes=scratch,
        compiler_params=pltpu.CompilerParams(vmem_limit_bytes=vmem),
        cost_estimate=pl.CostEstimate(flops=1000, bytes_accessed=1000, transcendentals=0),
    )(*operands)


def shaped(shape, kind):
    return jax.ShapeDtypeStruct(shape, kind)


def dot_nn(left, right):
    return lax.dot_general(left, right, (((1,), (0,)), ((), ())), preferred_element_type=F32)


def dot_nt(left, right):
    return lax.dot_general(left, right, (((1,), (1,)), ((), ())), preferred_element_type=F32)


def dot_tn(left, right):
    return lax.dot_general(left, right, (((0,), (0,)), ((), ())), preferred_element_type=F32)


def centre_scale(rows):
    centred = rows - jnp.mean(rows, -1, keepdims=True)
    inverse = lax.rsqrt(jnp.mean(centred * centred, -1, keepdims=True) + 1e-05)
    return centred * inverse, inverse


DIMS = (2, 4, 4)
STRIDES = (16, 4, 1)


def lat_swap(array, bits):
    count = lax.axis_size("lat")
    return lax.ppermute(array, "lat", [(i, i ^ bits) for i in range(count)])


def lon_swap(array, digit, bits):
    count = lax.axis_size("lon")
    return lax.ppermute(array, "lon", [(i, i ^ (bits * STRIDES[digit])) for i in range(count)])


def add_parts(*arrays):
    return sum(array.astype(F32) for array in arrays).astype(BF16)


def gather_mid(own, digit):
    pair = jnp.stack([own, lon_swap(own, digit, 1)])
    return pair, lon_swap(pair, digit, 3)


def gather_near(stacks, digit):
    first, second = stacks
    return (
        jnp.stack([first, lon_swap(first, digit, 1)]),
        jnp.stack([second, lon_swap(second, digit, 3)]),
    )


def gather_far(near, digit):
    return lon_swap(near[0], digit, 3), lon_swap(near[1], digit, 1)


def front_body(
    half_lat, flag_ref, x_ref, top_ref, bot_ref, left_ref, right_ref, scale_ref, qkv_w, out_w,
    merge_hbm, mask_ref, ones_ref, lane_ref, sums_ref, *refs,
):
    (
        skip_ref, cat_ref, coarse_ref, normed_ref,
        ext, xw, qkv, att, cat, catn, spread, merge_w, sem,
    ) = refs[-13:]
    levels, rows, cols, width = x_ref.shape
    fetch = pltpu.make_async_copy(merge_hbm, merge_w, sem)
    fetch.start()
    lead = 8
    half_lon = left_ref.shape[2]
    tokens = levels * WH * WW
    wins = (cols + 2 * half_lon) // WW

    def fill(row, carry):
        for l in range(levels):
            ext[l, half_lat + row, lead : lead + cols, :] = x_ref[l, row].astype(F32)
        return carry

    lax.fori_loop(0, rows, fill, 0)
    for l in range(levels):
        for r in range(half_lat):
            ext[l, r, lead : lead + cols, :] = top_ref[l, r].astype(F32)
            ext[l, half_lat + rows + r, lead : lead + cols, :] = bot_ref[l, r].astype(F32)

    def fill_sides(row, carry):
        for l in range(levels):
            ext[l, row, lead - half_lon : lead, :] = left_ref[l, row].astype(F32)
            ext[l, row, lead + cols : lead + cols + half_lon, :] = right_ref[l, row].astype(F32)
        return carry

    lax.fori_loop(0, rows + 2 * half_lat, fill_sides, 0)

    chunk = 256
    sections = width // chunk
    groups = width // (GROUP * HEAD)
    lanes = GROUP * HEAD

    def places():
        for c in range(wins):
            for l in range(levels):
                for r in range(WH):
                    yield c, l, r

    def band(b, carry):
        for c, l, r in places():
            at = c * tokens + (l * WH + r) * WW
            start = lead - half_lon + c * WW
            xw[at : at + WW, :] = ext[l, b * WH + r, start : start + WW, :]
        normed = centre_scale(xw[...])[0].astype(BF16)
        for j in range(3 * sections):
            y = dot_nn(normed, qkv_w[:, j * chunk : (j + 1) * chunk])
            if j < 2 * sections:
                square = y * y
                high = square.astype(BF16)
                low = (square - high.astype(F32)).astype(BF16)
                total = dot_nn(high, ones_ref[...]) + dot_nn(low, ones_ref[...])
                y = y * lax.rsqrt(total + 1e-06)
                if j < sections:
                    y = y * scale_ref[:, j * chunk : (j + 1) * chunk]
            qkv[:, j * chunk : (j + 1) * chunk] = y.astype(BF16)
        allowed = mask_ref[flag_ref[b]]
        for c in range(wins):
            rows_at = slice(c * tokens, (c + 1) * tokens)
            for g in range(groups):
                q = qkv[rows_at, g * lanes : (g + 1) * lanes]
                k = qkv[rows_at, width + g * lanes : width + (g + 1) * lanes]
                v = qkv[rows_at, 2 * width + g * lanes : 2 * width + (g + 1) * lanes]
                k4 = jnp.concatenate([k * lane_ref[h : h + 1, :] for h in range(GROUP)], 0)
                v4 = jnp.concatenate([v * lane_ref[h : h + 1, :] for h in range(GROUP)], 0)
                weight = jnp.exp2(dot_nt(q, k4)).astype(BF16) * allowed
                both = dot_nn(weight, jnp.concatenate([v4, sums_ref[...]], 1))
                att[rows_at, g * lanes : (g + 1) * lanes] = (
                    both[:, :lanes] / both[:, lanes:]
                ).astype(BF16)
        skip = xw[...] + dot_nn(att[...], out_w[...])
        xw[...] = skip.astype(BF16).astype(F32)
        for c, l, r in places():
            at = c * tokens + (l * WH + r) * WW
            start = lead - half_lon + c * WW
            ext[l, b * WH + r, start : start + WW, :] = xw[at : at + WW, :]
        return carry

    lax.fori_loop(0, (rows + 2 * half_lat) // WH, band, 0)

    def store_skip(row, carry):
        for l in range(levels):
            line = ext[l, half_lat + row, lead : lead + cols, :]
            skip_ref[l, row] = line.astype(BF16)
            for q in range(width // LANES):
                spread[l, row, q] = line[:, q * LANES : (q + 1) * LANES]
        return carry

    lax.fori_loop(0, rows, store_skip, 0)
    half = cols // 2
    for l in range(levels):
        for i in range(rows // 2):
            at = (l * (rows // 2) + i) * half
            for a in range(2):
                for b in range(2):
                    for q in range(width // LANES):
                        to = (a + 2 * b) * width + q * LANES
                        cat[at : at + half, to : to + LANES] = spread[
                            l, 2 * i + a, q, pl.ds(b, half, 2), :
                        ]
    total = cat.shape[0]
    step = 96
    for s in range(0, total, step):
        piece = cat[s : s + step, :]
        cat_ref[s : s + step, :] = piece.astype(BF16)
        catn[s : s + step, :] = centre_scale(piece)[0].astype(BF16)
    fetch.wait()
    coarse = dot_nn(catn[...], merge_w[...]).astype(BF16)
    coarse_ref[...] = coarse
    normed_ref[...] = centre_scale(coarse.astype(F32))[0].astype(BF16)


def front(fine, top, bot, left, right, head_scale, qkv_weight, out_weight, merge_weight, after):
    levels, rows, cols, width = fine.shape
    half_lat = WH // 2
    tokens = levels * WH * WW
    ext_rows = rows + 2 * half_lat
    bands = ext_rows // WH
    wins = (cols + WW) // WW
    heads = head_scale.shape[0]
    coarse_width = merge_weight.shape[1]
    coarse_tokens = levels * rows * cols // 4
    lat_place = lax.axis_index("lat")
    lat_last = lax.axis_size("lat") - 1
    band_ids = jnp.arange(bands)
    flags = (
        ((band_ids == 0) & (lat_place == 0)) | ((band_ids == bands - 1) & (lat_place == lat_last))
    ).astype(jnp.int32)
    scale = jnp.repeat(head_scale * (1.0 / math.log(2.0)), width // heads).reshape(1, width)
    group = (np.arange(tokens) // WW) % WH < half_lat
    same = np.tile(group[:, None] == group[None, :], (1, GROUP))
    mask = jnp.asarray(np.stack([np.ones_like(same), same]), BF16)
    lane_head = np.arange(256) // HEAD
    ones = jnp.asarray(lane_head[:, None] == lane_head[None, :], BF16)
    lane = jnp.asarray(np.arange(GROUP)[:, None] == lane_head[None, : GROUP * HEAD], BF16)
    sums = jnp.asarray(
        np.repeat(np.arange(GROUP), tokens)[:, None] == lane_head[None, : GROUP * HEAD], BF16
    )
    return run_kernel(
        functools.partial(front_body, half_lat),
        "front",
        [SCALARS] + [WHOLE] * 8 + [LEFT_OUT] + [WHOLE] * 4 + [LEFT_OUT] * len(after),
        [
            shaped((levels, rows, cols, width), BF16),
            shaped((coarse_tokens, 4 * width), BF16),
            shaped((coarse_tokens, coarse_width), BF16),
            shaped((coarse_tokens, coarse_width), BF16),
        ],
        [
            pltpu.VMEM((levels, ext_rows, cols + 16, width), F32),
            pltpu.VMEM((wins * tokens, width), F32),
            pltpu.VMEM((wins * tokens, 3 * width), BF16),
            pltpu.VMEM((wins * tokens, width), BF16),
            pltpu.VMEM((coarse_tokens, 4 * width), F32),
            pltpu.VMEM((coarse_tokens, 4 * width), BF16),
            pltpu.VMEM((levels, rows, width // LANES, cols, LANES), F32),
            pltpu.VMEM(merge_weight.shape, BF16),
            pltpu.SemaphoreType.DMA,
        ],
        30_000_000_000,
        12_000_000,
        flags, fine, top, bot, left, right, scale, qkv_weight, out_weight, merge_weight,
        mask, ones, lane, sums, *after,
        vmem=56 * MIB,
    )


def lay_blocks(place_ref, mid, last, near, far, dest):
    depth = dest.shape[0] // (DIMS[0] * DIMS[1] * DIMS[2])
    for stack, (mids, lasts) in enumerate((((0, 1), (0, 1, 3, 2)), ((3, 2), (0, 3, 1, 2)))):
        for at, k_last in enumerate(lasts):
            ref = near[stack] if at < 2 else far[stack]
            for m, k_mid in enumerate(mids):
                for k_first in range(DIMS[0]):
                    block = 0
                    for digit, k in ((0, k_first), (mid, k_mid), (last, k_last)):
                        block += jnp.bitwise_xor(place_ref[digit], k) * STRIDES[digit]
                    start = pl.multiple_of(block * depth, depth)
                    dest[pl.ds(start, depth), :] = ref[at % 2, m, k_first]


def prep_body(place_ref, *refs):
    up_parts, down_parts, cots = refs[:4], refs[4:8], refs[8:12]
    up_ref, up_t_ref, down_ref, near_ref, away_ref, down_t = refs[12:]
    lay_blocks(place_ref, 2, 1, up_parts[:2], up_parts[2:], up_ref)
    lay_blocks(place_ref, 1, 2, down_parts[:2], down_parts[2:], down_t)
    for j in range(4):
        n = cots[j].shape[0]
        grad_ref = near_ref if j < 2 else away_ref
        at = slice((j % 2) * n, (j % 2 + 1) * n)
        grad_ref[at, :] = dot_nn(cots[j][...], down_t[...]).astype(BF16)
    ff = up_ref.shape[1]
    step = 256
    for s in range(0, ff, step):
        up_t_ref[s : s + step, :] = up_ref[:, s : s + step].T
        down_ref[s : s + step, :] = down_t[:, s : s + step].T


def prep(place, up_parts, down_parts, cots):
    ff = up_parts[0].shape[-1]
    tokens, width = cots[0].shape
    return run_kernel(
        prep_body,
        "prep",
        [SCALARS] + [WHOLE] * 12,
        [
            shaped((width, ff), BF16),
            shaped((ff, width), BF16),
            shaped((ff, width), BF16),
            shaped((2 * tokens, ff), BF16),
            shaped((2 * tokens, ff), BF16),
        ],
        [pltpu.VMEM((width, ff), BF16)],
        8 * tokens * width * ff,
        12_000_000,
        place, *up_parts, *down_parts, *cots,
        vmem=56 * MIB,
    )


TERM_PARTS = (((0, 3), (0, 3)), ((1, 2), (0, 3)), ((0, 1), (1, 2)), ((3, 2), (1, 2)))


def term_into(held, place_ref, left, right, mid, last):
    width = left.shape[1]
    depth = held.shape[3]
    chunk = 256
    for s in range(0, width, chunk):
        total = dot_tn(left[:, s : s + chunk], right[...]).astype(BF16)
        for m in range(chunk // depth):
            block = s // depth + m
            k = [
                jnp.bitwise_xor(place_ref[digit], (block // STRIDES[digit]) % DIMS[digit])
                for digit in range(3)
            ]
            held[k[last], k[mid], k[0]] = total[m * depth : (m + 1) * depth, :]


def start_all(pairs, sems):
    copies = [pltpu.make_async_copy(a, b, sems.at[i]) for i, (a, b) in enumerate(pairs)]
    for copy in copies:
        copy.start()
    return copies


def activate(tokens, up, grads, hid, pre, rows):
    chunk = 256
    for s in range(0, up.shape[1], chunk):
        act = dot_nn(tokens, up[:, s : s + chunk])
        cdf = 0.5 + 0.5 * lax.erf(act * math.sqrt(0.5))
        hid[rows, s : s + chunk] = (act * cdf).astype(BF16)
        slope = cdf + act * (jnp.exp(-0.5 * (act * act)) * (1.0 / math.sqrt(2.0 * math.pi)))
        pre[rows, s : s + chunk] = (grads[rows, s : s + chunk].astype(F32) * slope).astype(BF16)


def near_body(first_ref, second_ref, grad_ref, up_ref, hid_ref, pre_ref):
    n = first_ref.shape[0]
    for j, tokens in enumerate((first_ref, second_ref)):
        activate(tokens[...], up_ref, grad_ref, hid_ref, pre_ref, slice(j * n, (j + 1) * n))


def feed_near(first, second, grads, up):
    n, width = first.shape
    ff = up.shape[1]
    return run_kernel(
        near_body,
        "feed_near",
        [WHOLE] * 4,
        [shaped((2 * n, ff), BF16)] * 2,
        [],
        0,
        0,
        first, second, grads, up,
        vmem=56 * MIB,
    )


def feed_body(place_ref, *refs):
    token_refs, cot_refs, refs = refs[:4], refs[4:8], refs[8:]
    (grad_hbm, hid_hbm, pre_hbm, up_hbm, up_t_hbm, down_hbm), refs = refs[:6], refs[6:]
    up_outs, down_outs, (near_hbm, away_hbm, send_hbm), refs = refs[:4], refs[4:8], refs[8:11], refs[11:]
    tok, cot, grads, up, up_t, down, hid, pre, held_u, held_d, near, away, send, ins, outs = refs
    n = token_refs[0].shape[0]
    first = pl.ds(0, 2 * n)
    pairs = [(up_hbm, up), (grad_hbm, grads)]
    pairs += [(token_refs[j], tok.at[pl.ds(j * n, n)]) for j in (2, 3)]
    pairs += [(hid_hbm, hid.at[first])]
    pairs += [(cot_refs[j], cot.at[pl.ds(j * n, n)]) for j in range(4)]
    pairs += [(token_refs[j], tok.at[pl.ds(j * n, n)]) for j in (0, 1)]
    pairs += [(pre_hbm, pre.at[first]), (up_t_hbm, up_t), (down_hbm, down)]
    fetches = start_all(pairs, ins)
    stores = []

    def store(src, dst):
        copy = pltpu.make_async_copy(src, dst, outs.at[len(stores)])
        copy.start()
        stores.append(copy)

    for k in range(4):
        fetches[k].wait()
    far = pl.ds(2 * n, 2 * n)
    for j in (2, 3):
        rows = slice((j - 2) * n, (j - 1) * n)
        activate(tok[j * n : (j + 1) * n, :], up, grads, hid.at[far], pre.at[far], rows)
    for k in range(4, 9):
        fetches[k].wait()
    for held, left, right, parts, mid, last in (
        (held_d, cot, hid, down_outs, 1, 2),
        (held_u, tok, pre, up_outs, 2, 1),
    ):
        if held is held_u:
            for k in range(9, 12):
                fetches[k].wait()
        term_into(held, place_ref, left, right, mid, last)
        for out, (lasts, mids) in zip(parts, TERM_PARTS):
            for i, k_last in enumerate(lasts):
                for m, k_mid in enumerate(mids):
                    store(held.at[k_last, k_mid], out.at[i, m])
    for which, (rows, weight) in enumerate(((pre, up_t), (hid, down))):
        fetches[12 + which].wait()
        for side, (keep, keep_hbm) in enumerate(((near, near_hbm), (away, away_hbm))):
            sums = dot_nn(rows[2 * side * n : 2 * (side + 1) * n, :], weight[...]).astype(BF16)
            keep[which] = sums[:n]
            send[2 * side + which] = sums[n:]
            store(keep.at[which], keep_hbm.at[which])
            store(send.at[2 * side + which], send_hbm.at[2 * side + which])
    for copy in stores:
        copy.wait()


def feed(place, tokens, cots, grads, near_hid, near_pre, up, up_t, down):
    n, width = tokens[0].shape
    ff = up.shape[1]
    depth = width // (DIMS[0] * DIMS[1] * DIMS[2])
    part = shaped((2, 2, DIMS[0], depth, ff), BF16)
    outs = [part] * 8 + [shaped((k, n, width), BF16) for k in (2, 2, 4)]
    result = pl.pallas_call(
        feed_body,
        name="feed",
        in_specs=[SCALARS] + [LEFT_OUT] * 14,
        out_specs=[LEFT_OUT] * len(outs),
        out_shape=outs,
        scratch_shapes=[
            pltpu.VMEM((4 * n, width), BF16),
            pltpu.VMEM((4 * n, width), BF16),
            pltpu.VMEM((2 * n, ff), BF16),
            pltpu.VMEM((width, ff), BF16),
            pltpu.VMEM((ff, width), BF16),
            pltpu.VMEM((ff, width), BF16),
            pltpu.VMEM((4 * n, ff), BF16),
            pltpu.VMEM((4 * n, ff), BF16),
            pltpu.VMEM((4, 4, DIMS[0], depth, ff), BF16),
            pltpu.VMEM((4, 4, DIMS[0], depth, ff), BF16),
            pltpu.VMEM((2, n, width), BF16),
            pltpu.VMEM((2, n, width), BF16),
            pltpu.VMEM((4, n, width), BF16),
            pltpu.SemaphoreType.DMA((14,)),
            pltpu.SemaphoreType.DMA((40,)),
        ],
        compiler_params=pltpu.CompilerParams(vmem_limit_bytes=56 * MIB),
        cost_estimate=pl.CostEstimate(flops=1000, bytes_accessed=1000, transcendentals=0),
    )(place, *tokens, *cots, grads, near_hid, near_pre, up, up_t, down)
    return result[:4], result[4:8], result[8:]


def last_body(coarse_ref, cot_ref, own_ref, there_ref, far_ref, cat_ref, merge_ref, *refs):
    skip_grad, slots, spread, shares, sems = refs[-5:]
    fetches = [
        pltpu.make_async_copy(ref.at[0], shares.at[k], sems.at[k])
        for k, ref in enumerate((own_ref, there_ref))
    ]
    for fetch in fetches:
        fetch.start()
    levels, rows, cols, width = skip_grad.shape
    coarse = coarse_ref[...].astype(F32)
    normed, inverse = centre_scale(coarse)
    for fetch in fetches:
        fetch.wait()
    grad = shares[0].astype(F32) + shares[1].astype(F32) + far_ref[...].astype(F32)
    back = inverse * (
        grad
        - jnp.mean(grad, -1, keepdims=True)
        - normed * jnp.mean(grad * normed, -1, keepdims=True)
    )
    coarse_grad = (cot_ref[...].astype(F32) + back).astype(BF16)
    slots[...] = dot_nt(coarse_grad, merge_ref[...])
    half = cols // 2
    step = 96
    for s in range(0, slots.shape[0], step):
        normed, inverse = centre_scale(cat_ref[s : s + step, :].astype(F32))
        grad = slots[s : s + step, :]
        slots[s : s + step, :] = inverse * (
            grad
            - jnp.mean(grad, -1, keepdims=True)
            - normed * jnp.mean(grad * normed, -1, keepdims=True)
        )
    for l in range(levels):
        for i in range(rows // 2):
            at = (l * (rows // 2) + i) * half
            for a in range(2):
                for b in range(2):
                    for q in range(width // LANES):
                        to = (a + 2 * b) * width + q * LANES
                        spread[l, 2 * i + a, q, pl.ds(b, half, 2), :] = slots[
                            at : at + half, to : to + LANES
                        ]

    def lay_out(row, carry):
        for l in range(levels):
            for q in range(width // LANES):
                skip_grad[l, row, :, q * LANES : (q + 1) * LANES] = spread[l, row, q]
        return carry

    lax.fori_loop(0, rows, lay_out, 0)


def last(coarse, cot, own, there, far, cat, merge_weight, fine_shape, after):
    levels, rows, cols, width = fine_shape
    return run_kernel(
        last_body,
        "last",
        [WHOLE] * 2 + [LEFT_OUT] * 2 + [WHOLE] * 3 + [LEFT_OUT] * len(after),
        [shaped(fine_shape, F32)],
        [
            pltpu.VMEM(cat.shape, F32),
            pltpu.VMEM((levels, rows, width // LANES, cols, LANES), F32),
            pltpu.VMEM((2, *own.shape[1:]), BF16),
            pltpu.SemaphoreType.DMA((2,)),
        ],
        2 * cat.shape[0] * merge_weight.shape[0] * merge_weight.shape[1],
        10_000_000,
        coarse, cot, own, there, far, cat, merge_weight, *after,
        vmem=30 * MIB,
    )[0]


def with_rows(cells, width):
    count = lax.axis_size("lat")
    above = lax.ppermute(
        cells[:, -width:], "lat", [(i, (i + 1) % count) for i in range(count)]
    )
    below = lax.ppermute(cells[:, :width], "lat", [((i + 1) % count, i) for i in range(count)])
    return above, below


def on_device(
    fine_field, head_scale, qkv_weight, out_weight, merge_weight, up_weight, down_weight, cotangent
):
    levels, lat_rows, lon_cols, channels = fine_field.shape
    coarse_width = merge_weight.shape[1]
    half_lat, half_lon = WH // 2, WW // 2
    lon_count = lax.axis_size("lon")
    me = lax.axis_index("lon")
    place = jnp.stack([(me // STRIDES[d]) % DIMS[d] for d in range(3)]).astype(jnp.int32)

    weights = jnp.stack([up_weight, down_weight.T])[:, None]
    weights = jnp.concatenate([weights, lon_swap(weights, 0, 1)], 1)
    top, bot = with_rows(fine_field, half_lat)
    tall = [
        jnp.concatenate([top[:, :, cut], fine_field[:, :, cut], bot[:, :, cut]], 1)
        for cut in (slice(lon_cols - half_lon, lon_cols), slice(0, half_lon))
    ]
    left = lax.ppermute(tall[0], "lon", [(i, (i + 1) % lon_count) for i in range(lon_count)])
    right = lax.ppermute(tall[1], "lon", [((i + 1) % lon_count, i) for i in range(lon_count)])
    up_near = gather_near(gather_mid(weights[0], 2), 1)
    down_near = gather_near(gather_mid(weights[1], 1), 2)
    cot = cotangent.reshape(-1, coarse_width)
    held, _, _ = lax.optimization_barrier((cot, left, right))
    cot_c, cot_y = lat_swap(held, 1), lat_swap(held, 2)
    left, right, _, _, _ = lax.optimization_barrier((left, right, up_near, down_near, cot_c))
    skip_field, cat, coarse, normed = front(
        fine_field, top, bot, left, right, head_scale, qkv_weight, out_weight, merge_weight, ()
    )
    up_far, down_far = gather_far(up_near, 1), gather_far(down_near, 2)
    normed, up_far, down_far, cot_y = lax.optimization_barrier((normed, up_far, down_far, cot_y))
    cots = [cot, cot_c, cot_y, lat_swap(cot_y, 1)]
    normed_c, normed_y = lat_swap(normed, 1), lat_swap(normed, 2)
    up, up_t, down, near_grad, away_grad = prep(
        place, (*up_near, *up_far), (*down_near, *down_far), cots
    )
    near_hid, near_pre = feed_near(normed, normed_c, near_grad, up)
    normed_y, near_hid = lax.optimization_barrier((normed_y, near_hid))
    tokens = [normed, normed_c, normed_y, lat_swap(normed_y, 1)]

    def scatter_one(parts, digit):
        return lon_swap(parts[1], digit, 1), lon_swap(parts[3], digit, 3)

    def scatter_two(parts, came, digit):
        keep = [add_parts(parts[2 * h][0], came[h][0]) for h in range(2)]
        send = [add_parts(parts[2 * h][1], came[h][1]) for h in range(2)]
        return keep, send, (lon_swap(send[0], digit, 3), lon_swap(send[1], digit, 1))

    term_up, term_down, (near, away, send) = feed(
        place, tokens, cots, away_grad, near_hid, near_pre, up, up_t, down
    )
    there = lat_swap(send, 1)
    up_came, down_came = scatter_one(term_up, 1), scatter_one(term_down, 2)
    back_pass = add_parts(away[0], there[2])
    back_far = lat_swap(back_pass, 2)
    up_came, down_came, back_pass = lax.optimization_barrier((up_came, down_came, back_pass))
    up_keep, _, up_came = scatter_two(term_up, up_came, 1)
    down_keep, _, down_came = scatter_two(term_down, down_came, 2)
    up_halves = [add_parts(up_keep[h], up_came[h]) for h in range(2)]
    down_halves = [add_parts(down_keep[h], down_came[h]) for h in range(2)]
    up_came, down_came = lon_swap(up_halves[1], 2, 1), lon_swap(down_halves[1], 1, 1)
    out_pass = add_parts(away[1], there[3])
    out_far = lat_swap(out_pass, 2)
    held, up_halves, down_halves = lax.optimization_barrier((coarse, up_halves, down_halves))
    skip_grad = last(held, cot, near, there, back_far, cat, merge_weight, fine_field.shape, ())
    up_came, down_came, skip_grad = lax.optimization_barrier((up_came, down_came, skip_grad))
    up_pair, down_pair = add_parts(up_halves[0], up_came), add_parts(down_halves[0], down_came)
    up_end = add_parts(up_pair[0], lon_swap(up_pair[1], 2, 3))
    down_end = add_parts(down_pair[0], lon_swap(down_pair[1], 1, 3))
    both = jnp.stack([up_end, down_end], 1)
    both = both[0].astype(F32) + lon_swap(both[1], 0, 1).astype(F32)
    coarse_out = (
        coarse.astype(F32)
        + (near[1].astype(F32) + there[1].astype(F32) + out_far.astype(F32))
    ).astype(BF16)
    return (
        skip_field,
        coarse_out.reshape(levels, lat_rows // 2, lon_cols // 2, coarse_width),
        both[0],
        both[1].T,
        skip_grad,
    )


def solution(mesh):
    placed = (
        P(None, "lat", "lon", None),
        P(),
        P(),
        P(),
        P(),
        P("lon", "lat"),
        P("lat", "lon"),
        P(None, "lat", "lon", None),
    )
    return jax.shard_map(
        on_device,
        mesh=mesh,
        in_specs=placed,
        out_specs=(
            P(None, "lat", "lon", None),
            P(None, "lat", "lon", None),
            P("lon", "lat"),
            P("lat", "lon"),
            P(None, "lat", "lon", None),
        ),
        check_vma=False,
    )
```

```python
import functools
import math

import jax
import jax.numpy as jnp
import numpy as np
from jax import lax
from jax.experimental import pallas as pl
from jax.experimental.pallas import tpu as pltpu
from jax.sharding import PartitionSpec as P

WH = 6
WW = 12
HEAD = 32
LANES = 128
GROUP = 4
F32 = jnp.float32
BF16 = jnp.bfloat16
MIB = 1024 * 1024

WHOLE = pl.BlockSpec(memory_space=pltpu.VMEM)
SCALARS = pl.BlockSpec(memory_space=pltpu.SMEM)
LEFT_OUT = pl.BlockSpec(memory_space=pl.ANY)


def run_kernel(body, name, specs, outs, scratch, flops, moved, *operands, vmem):
    return pl.pallas_call(
        body,
        name=name,
        in_specs=specs,
        out_specs=[WHOLE] * len(outs),
        out_shape=outs,
        scratch_shapes=scratch,
        compiler_params=pltpu.CompilerParams(vmem_limit_bytes=vmem),
        cost_estimate=pl.CostEstimate(flops=1000, bytes_accessed=1000, transcendentals=0),
    )(*operands)


def shaped(shape, kind):
    return jax.ShapeDtypeStruct(shape, kind)


def dot_nn(left, right):
    return lax.dot_general(left, right, (((1,), (0,)), ((), ())), preferred_element_type=F32)


def dot_nt(left, right):
    return lax.dot_general(left, right, (((1,), (1,)), ((), ())), preferred_element_type=F32)


def dot_tn(left, right):
    return lax.dot_general(left, right, (((0,), (0,)), ((), ())), preferred_element_type=F32)


def centre_scale(rows):
    centred = rows - jnp.mean(rows, -1, keepdims=True)
    inverse = lax.rsqrt(jnp.mean(centred * centred, -1, keepdims=True) + 1e-05)
    return centred * inverse, inverse


DIMS = (2, 4, 4)
STRIDES = (16, 4, 1)


def lat_swap(array, bits):
    count = lax.axis_size("lat")
    return lax.ppermute(array, "lat", [(i, i ^ bits) for i in range(count)])


def lon_swap(array, digit, bits):
    count = lax.axis_size("lon")
    return lax.ppermute(array, "lon", [(i, i ^ (bits * STRIDES[digit])) for i in range(count)])


def add_parts(*arrays):
    return sum(array.astype(F32) for array in arrays).astype(BF16)


def gather_mid(own, digit):
    pair = jnp.stack([own, lon_swap(own, digit, 1)])
    return pair, lon_swap(pair, digit, 3)


def gather_near(stacks, digit):
    first, second = stacks
    return (
        jnp.stack([first, lon_swap(first, digit, 1)]),
        jnp.stack([second, lon_swap(second, digit, 3)]),
    )


def gather_far(near, digit):
    return lon_swap(near[0], digit, 3), lon_swap(near[1], digit, 1)


def front_body(
    half_lat, flag_ref, x_ref, top_ref, bot_ref, left_ref, right_ref, scale_ref, qkv_w, out_w,
    merge_hbm, mask_ref, ones_ref, lane_ref, sums_ref, *refs,
):
    (
        skip_ref, cat_ref, coarse_ref, normed_ref,
        ext, xw, qkv, att, cat, catn, spread, merge_w, sem,
    ) = refs[-13:]
    levels, rows, cols, width = x_ref.shape
    fetch = pltpu.make_async_copy(merge_hbm, merge_w, sem)
    fetch.start()
    lead = 8
    half_lon = left_ref.shape[2]
    tokens = levels * WH * WW
    wins = (cols + 2 * half_lon) // WW

    def fill(row, carry):
        for l in range(levels):
            ext[l, half_lat + row, lead : lead + cols, :] = x_ref[l, row].astype(F32)
        return carry

    lax.fori_loop(0, rows, fill, 0)
    for l in range(levels):
        for r in range(half_lat):
            ext[l, r, lead : lead + cols, :] = top_ref[l, r].astype(F32)
            ext[l, half_lat + rows + r, lead : lead + cols, :] = bot_ref[l, r].astype(F32)

    def fill_sides(row, carry):
        for l in range(levels):
            ext[l, row, lead - half_lon : lead, :] = left_ref[l, row].astype(F32)
            ext[l, row, lead + cols : lead + cols + half_lon, :] = right_ref[l, row].astype(F32)
        return carry

    lax.fori_loop(0, rows + 2 * half_lat, fill_sides, 0)

    chunk = 256
    sections = width // chunk
    groups = width // (GROUP * HEAD)
    lanes = GROUP * HEAD

    def places():
        for c in range(wins):
            for l in range(levels):
                for r in range(WH):
                    yield c, l, r

    def band(b, carry):
        for c, l, r in places():
            at = c * tokens + (l * WH + r) * WW
            start = lead - half_lon + c * WW
            xw[at : at + WW, :] = ext[l, b * WH + r, start : start + WW, :]
        normed = centre_scale(xw[...])[0].astype(BF16)
        for j in range(3 * sections):
            y = dot_nn(normed, qkv_w[:, j * chunk : (j + 1) * chunk])
            if j < 2 * sections:
                square = y * y
                high = square.astype(BF16)
                low = (square - high.astype(F32)).astype(BF16)
                total = dot_nn(high, ones_ref[...]) + dot_nn(low, ones_ref[...])
                y = y * lax.rsqrt(total + 1e-06)
                if j < sections:
                    y = y * scale_ref[:, j * chunk : (j + 1) * chunk]
            qkv[:, j * chunk : (j + 1) * chunk] = y.astype(BF16)
        allowed = mask_ref[flag_ref[b]]
        for c in range(wins):
            rows_at = slice(c * tokens, (c + 1) * tokens)
            for g in range(groups):
                q = qkv[rows_at, g * lanes : (g + 1) * lanes]
                k = qkv[rows_at, width + g * lanes : width + (g + 1) * lanes]
                v = qkv[rows_at, 2 * width + g * lanes : 2 * width + (g + 1) * lanes]
                k4 = jnp.concatenate([k * lane_ref[h : h + 1, :] for h in range(GROUP)], 0)
                v4 = jnp.concatenate([v * lane_ref[h : h + 1, :] for h in range(GROUP)], 0)
                weight = jnp.exp2(dot_nt(q, k4)).astype(BF16) * allowed
                both = dot_nn(weight, jnp.concatenate([v4, sums_ref[...]], 1))
                att[rows_at, g * lanes : (g + 1) * lanes] = (
                    both[:, :lanes] / both[:, lanes:]
                ).astype(BF16)
        skip = xw[...] + dot_nn(att[...], out_w[...])
        xw[...] = skip.astype(BF16).astype(F32)
        for c, l, r in places():
            at = c * tokens + (l * WH + r) * WW
            start = lead - half_lon + c * WW
            ext[l, b * WH + r, start : start + WW, :] = xw[at : at + WW, :]
        return carry

    lax.fori_loop(0, (rows + 2 * half_lat) // WH, band, 0)

    def store_skip(row, carry):
        for l in range(levels):
            line = ext[l, half_lat + row, lead : lead + cols, :]
            skip_ref[l, row] = line.astype(BF16)
            for q in range(width // LANES):
                spread[l, row, q] = line[:, q * LANES : (q + 1) * LANES]
        return carry

    lax.fori_loop(0, rows, store_skip, 0)
    half = cols // 2
    for l in range(levels):
        for i in range(rows // 2):
            at = (l * (rows // 2) + i) * half
            for a in range(2):
                for b in range(2):
                    for q in range(width // LANES):
                        to = (a + 2 * b) * width + q * LANES
                        cat[at : at + half, to : to + LANES] = spread[
                            l, 2 * i + a, q, pl.ds(b, half, 2), :
                        ]
    total = cat.shape[0]
    step = 96
    for s in range(0, total, step):
        piece = cat[s : s + step, :]
        cat_ref[s : s + step, :] = piece.astype(BF16)
        catn[s : s + step, :] = centre_scale(piece)[0].astype(BF16)
    fetch.wait()
    coarse = dot_nn(catn[...], merge_w[...]).astype(BF16)
    coarse_ref[...] = coarse
    normed_ref[...] = centre_scale(coarse.astype(F32))[0].astype(BF16)


def front(fine, top, bot, left, right, head_scale, qkv_weight, out_weight, merge_weight, after):
    levels, rows, cols, width = fine.shape
    half_lat = WH // 2
    tokens = levels * WH * WW
    ext_rows = rows + 2 * half_lat
    bands = ext_rows // WH
    wins = (cols + WW) // WW
    heads = head_scale.shape[0]
    coarse_width = merge_weight.shape[1]
    coarse_tokens = levels * rows * cols // 4
    lat_place = lax.axis_index("lat")
    lat_last = lax.axis_size("lat") - 1
    band_ids = jnp.arange(bands)
    flags = (
        ((band_ids == 0) & (lat_place == 0)) | ((band_ids == bands - 1) & (lat_place == lat_last))
    ).astype(jnp.int32)
    scale = jnp.repeat(head_scale * (1.0 / math.log(2.0)), width // heads).reshape(1, width)
    group = (np.arange(tokens) // WW) % WH < half_lat
    same = np.tile(group[:, None] == group[None, :], (1, GROUP))
    mask = jnp.asarray(np.stack([np.ones_like(same), same]), BF16)
    lane_head = np.arange(256) // HEAD
    ones = jnp.asarray(lane_head[:, None] == lane_head[None, :], BF16)
    lane = jnp.asarray(np.arange(GROUP)[:, None] == lane_head[None, : GROUP * HEAD], BF16)
    sums = jnp.asarray(
        np.repeat(np.arange(GROUP), tokens)[:, None] == lane_head[None, : GROUP * HEAD], BF16
    )
    return run_kernel(
        functools.partial(front_body, half_lat),
        "front",
        [SCALARS] + [WHOLE] * 8 + [LEFT_OUT] + [WHOLE] * 4 + [LEFT_OUT] * len(after),
        [
            shaped((levels, rows, cols, width), BF16),
            shaped((coarse_tokens, 4 * width), BF16),
            shaped((coarse_tokens, coarse_width), BF16),
            shaped((coarse_tokens, coarse_width), BF16),
        ],
        [
            pltpu.VMEM((levels, ext_rows, cols + 16, width), F32),
            pltpu.VMEM((wins * tokens, width), F32),
            pltpu.VMEM((wins * tokens, 3 * width), BF16),
            pltpu.VMEM((wins * tokens, width), BF16),
            pltpu.VMEM((coarse_tokens, 4 * width), F32),
            pltpu.VMEM((coarse_tokens, 4 * width), BF16),
            pltpu.VMEM((levels, rows, width // LANES, cols, LANES), F32),
            pltpu.VMEM(merge_weight.shape, BF16),
            pltpu.SemaphoreType.DMA,
        ],
        30_000_000_000,
        12_000_000,
        flags, fine, top, bot, left, right, scale, qkv_weight, out_weight, merge_weight,
        mask, ones, lane, sums, *after,
        vmem=56 * MIB,
    )


def lay_blocks(place_ref, mid, last, near, far, dest):
    depth = dest.shape[0] // (DIMS[0] * DIMS[1] * DIMS[2])
    for stack, (mids, lasts) in enumerate((((0, 1), (0, 1, 3, 2)), ((3, 2), (0, 3, 1, 2)))):
        for at, k_last in enumerate(lasts):
            ref = near[stack] if at < 2 else far[stack]
            for m, k_mid in enumerate(mids):
                for k_first in range(DIMS[0]):
                    block = 0
                    for digit, k in ((0, k_first), (mid, k_mid), (last, k_last)):
                        block += jnp.bitwise_xor(place_ref[digit], k) * STRIDES[digit]
                    start = pl.multiple_of(block * depth, depth)
                    dest[pl.ds(start, depth), :] = ref[at % 2, m, k_first]


def prep_body(place_ref, *refs):
    up_parts, down_parts, cots = refs[:4], refs[4:8], refs[8:12]
    up_hbm, up_t_hbm, down_hbm, near_hbm, away_hbm = refs[12:17]
    up_ref, up_t_ref, down_ref, near_ref, away_ref, down_t, sems = refs[17:]
    ff = up_ref.shape[1]
    step = 256
    stores = []

    def store(src, dst):
        copy = pltpu.make_async_copy(src, dst, sems.at[len(stores)])
        copy.start()
        stores.append(copy)

    lay_blocks(place_ref, 2, 1, up_parts[:2], up_parts[2:], up_ref)
    store(up_ref, up_hbm)
    lay_blocks(place_ref, 1, 2, down_parts[:2], down_parts[2:], down_t)
    for s in range(0, ff, step):
        up_t_ref[s : s + step, :] = up_ref[:, s : s + step].T
        down_ref[s : s + step, :] = down_t[:, s : s + step].T
    store(up_t_ref, up_t_hbm)
    store(down_ref, down_hbm)
    for grad_ref, grad_hbm, first in ((near_ref, near_hbm, 0), (away_ref, away_hbm, 2)):
        for j in range(2):
            n = cots[first + j].shape[0]
            grad_ref[j * n : (j + 1) * n, :] = dot_nn(
                cots[first + j][...], down_t[...]
            ).astype(BF16)
        store(grad_ref, grad_hbm)
    for copy in stores:
        copy.wait()


def prep(place, up_parts, down_parts, cots):
    ff = up_parts[0].shape[-1]
    tokens, width = cots[0].shape
    outs = [(width, ff), (ff, width), (ff, width), (2 * tokens, ff), (2 * tokens, ff)]
    return pl.pallas_call(
        prep_body,
        name="prep",
        in_specs=[SCALARS] + [WHOLE] * 12,
        out_specs=[LEFT_OUT] * 5,
        out_shape=[shaped(out, BF16) for out in outs],
        scratch_shapes=[pltpu.VMEM(out, BF16) for out in outs]
        + [pltpu.VMEM((width, ff), BF16), pltpu.SemaphoreType.DMA((5,))],
        compiler_params=pltpu.CompilerParams(vmem_limit_bytes=56 * MIB),
        cost_estimate=pl.CostEstimate(flops=1000, bytes_accessed=1000, transcendentals=0),
    )(place, *up_parts, *down_parts, *cots)


TERM_PARTS = (((0, 3), (0, 3)), ((1, 2), (0, 3)), ((0, 1), (1, 2)), ((3, 2), (1, 2)))


def term_into(held, place_ref, left, right, mid, last):
    width = left.shape[1]
    depth = held.shape[3]
    chunk = 256
    for s in range(0, width, chunk):
        total = dot_tn(left[:, s : s + chunk], right[...]).astype(BF16)
        for m in range(chunk // depth):
            block = s // depth + m
            k = [
                jnp.bitwise_xor(place_ref[digit], (block // STRIDES[digit]) % DIMS[digit])
                for digit in range(3)
            ]
            held[k[last], k[mid], k[0]] = total[m * depth : (m + 1) * depth, :]


def start_all(pairs, sems):
    copies = [pltpu.make_async_copy(a, b, sems.at[i]) for i, (a, b) in enumerate(pairs)]
    for copy in copies:
        copy.start()
    return copies


def activate(tokens, up, grads, hid, pre, rows):
    chunk = 256
    for s in range(0, up.shape[1], chunk):
        act = dot_nn(tokens, up[:, s : s + chunk])
        cdf = 0.5 + 0.5 * lax.erf(act * math.sqrt(0.5))
        hid[rows, s : s + chunk] = (act * cdf).astype(BF16)
        slope = cdf + act * (jnp.exp(-0.5 * (act * act)) * (1.0 / math.sqrt(2.0 * math.pi)))
        pre[rows, s : s + chunk] = (grads[rows, s : s + chunk].astype(F32) * slope).astype(BF16)


def near_body(first_ref, second_ref, grad_ref, up_ref, hid_ref, pre_ref):
    n = first_ref.shape[0]
    for j, tokens in enumerate((first_ref, second_ref)):
        activate(tokens[...], up_ref, grad_ref, hid_ref, pre_ref, slice(j * n, (j + 1) * n))


def feed_near(first, second, grads, up):
    n, width = first.shape
    ff = up.shape[1]
    return run_kernel(
        near_body,
        "feed_near",
        [WHOLE] * 4,
        [shaped((2 * n, ff), BF16)] * 2,
        [],
        0,
        0,
        first, second, grads, up,
        vmem=56 * MIB,
    )


def feed_body(place_ref, *refs):
    token_refs, cot_refs, refs = refs[:4], refs[4:8], refs[8:]
    (grad_hbm, hid_hbm, pre_hbm, up_hbm, up_t_hbm, down_hbm), refs = refs[:6], refs[6:]
    up_outs, down_outs, (near_hbm, away_hbm, send_hbm), refs = refs[:4], refs[4:8], refs[8:11], refs[11:]
    tok, cot, grads, up, up_t, down, hid, pre, held_u, held_d, near, away, send, ins, outs = refs
    n = token_refs[0].shape[0]
    first = pl.ds(0, 2 * n)
    pairs = [(up_hbm, up), (grad_hbm, grads)]
    pairs += [(token_refs[j], tok.at[pl.ds(j * n, n)]) for j in (2, 3)]
    pairs += [(hid_hbm, hid.at[first])]
    pairs += [(cot_refs[j], cot.at[pl.ds(j * n, n)]) for j in range(4)]
    pairs += [(token_refs[j], tok.at[pl.ds(j * n, n)]) for j in (0, 1)]
    pairs += [(pre_hbm, pre.at[first]), (up_t_hbm, up_t), (down_hbm, down)]
    fetches = start_all(pairs, ins)
    stores = []

    def store(src, dst):
        copy = pltpu.make_async_copy(src, dst, outs.at[len(stores)])
        copy.start()
        stores.append(copy)

    for k in range(4):
        fetches[k].wait()
    far = pl.ds(2 * n, 2 * n)
    for j in (2, 3):
        rows = slice((j - 2) * n, (j - 1) * n)
        activate(tok[j * n : (j + 1) * n, :], up, grads, hid.at[far], pre.at[far], rows)
    for k in range(4, 9):
        fetches[k].wait()
    for held, left, right, parts, mid, last in (
        (held_d, cot, hid, down_outs, 1, 2),
        (held_u, tok, pre, up_outs, 2, 1),
    ):
        if held is held_u:
            for k in range(9, 12):
                fetches[k].wait()
        term_into(held, place_ref, left, right, mid, last)
        for out, (lasts, mids) in zip(parts, TERM_PARTS):
            for i, k_last in enumerate(lasts):
                for m, k_mid in enumerate(mids):
                    store(held.at[k_last, k_mid], out.at[i, m])
    for which, (rows, weight) in enumerate(((pre, up_t), (hid, down))):
        fetches[12 + which].wait()
        for side, (keep, keep_hbm) in enumerate(((near, near_hbm), (away, away_hbm))):
            sums = dot_nn(rows[2 * side * n : 2 * (side + 1) * n, :], weight[...]).astype(BF16)
            keep[which] = sums[:n]
            send[2 * side + which] = sums[n:]
            store(keep.at[which], keep_hbm.at[which])
            store(send.at[2 * side + which], send_hbm.at[2 * side + which])
    for copy in stores:
        copy.wait()


def feed(place, tokens, cots, grads, near_hid, near_pre, up, up_t, down):
    n, width = tokens[0].shape
    ff = up.shape[1]
    depth = width // (DIMS[0] * DIMS[1] * DIMS[2])
    part = shaped((2, 2, DIMS[0], depth, ff), BF16)
    outs = [part] * 8 + [shaped((k, n, width), BF16) for k in (2, 2, 4)]
    result = pl.pallas_call(
        feed_body,
        name="feed",
        in_specs=[SCALARS] + [LEFT_OUT] * 14,
        out_specs=[LEFT_OUT] * len(outs),
        out_shape=outs,
        scratch_shapes=[
            pltpu.VMEM((4 * n, width), BF16),
            pltpu.VMEM((4 * n, width), BF16),
            pltpu.VMEM((2 * n, ff), BF16),
            pltpu.VMEM((width, ff), BF16),
            pltpu.VMEM((ff, width), BF16),
            pltpu.VMEM((ff, width), BF16),
            pltpu.VMEM((4 * n, ff), BF16),
            pltpu.VMEM((4 * n, ff), BF16),
            pltpu.VMEM((4, 4, DIMS[0], depth, ff), BF16),
            pltpu.VMEM((4, 4, DIMS[0], depth, ff), BF16),
            pltpu.VMEM((2, n, width), BF16),
            pltpu.VMEM((2, n, width), BF16),
            pltpu.VMEM((4, n, width), BF16),
            pltpu.SemaphoreType.DMA((14,)),
            pltpu.SemaphoreType.DMA((40,)),
        ],
        compiler_params=pltpu.CompilerParams(vmem_limit_bytes=56 * MIB),
        cost_estimate=pl.CostEstimate(flops=1000, bytes_accessed=1000, transcendentals=0),
    )(place, *tokens, *cots, grads, near_hid, near_pre, up, up_t, down)
    return result[:4], result[4:8], result[8:]


def last_body(coarse_ref, cot_ref, own_ref, there_ref, far_ref, cat_ref, merge_ref, *refs):
    skip_grad, slots, spread, shares, sems = refs[-5:]
    fetches = [
        pltpu.make_async_copy(ref.at[0], shares.at[k], sems.at[k])
        for k, ref in enumerate((own_ref, there_ref))
    ]
    for fetch in fetches:
        fetch.start()
    levels, rows, cols, width = skip_grad.shape
    coarse = coarse_ref[...].astype(F32)
    normed, inverse = centre_scale(coarse)
    for fetch in fetches:
        fetch.wait()
    grad = shares[0].astype(F32) + shares[1].astype(F32) + far_ref[...].astype(F32)
    back = inverse * (
        grad
        - jnp.mean(grad, -1, keepdims=True)
        - normed * jnp.mean(grad * normed, -1, keepdims=True)
    )
    coarse_grad = (cot_ref[...].astype(F32) + back).astype(BF16)
    slots[...] = dot_nt(coarse_grad, merge_ref[...])
    half = cols // 2
    step = 96
    for s in range(0, slots.shape[0], step):
        normed, inverse = centre_scale(cat_ref[s : s + step, :].astype(F32))
        grad = slots[s : s + step, :]
        slots[s : s + step, :] = inverse * (
            grad
            - jnp.mean(grad, -1, keepdims=True)
            - normed * jnp.mean(grad * normed, -1, keepdims=True)
        )
    for l in range(levels):
        for i in range(rows // 2):
            at = (l * (rows // 2) + i) * half
            for a in range(2):
                for b in range(2):
                    for q in range(width // LANES):
                        to = (a + 2 * b) * width + q * LANES
                        spread[l, 2 * i + a, q, pl.ds(b, half, 2), :] = slots[
                            at : at + half, to : to + LANES
                        ]

    def lay_out(row, carry):
        for l in range(levels):
            for q in range(width // LANES):
                skip_grad[l, row, :, q * LANES : (q + 1) * LANES] = spread[l, row, q]
        return carry

    lax.fori_loop(0, rows, lay_out, 0)


def last(coarse, cot, own, there, far, cat, merge_weight, fine_shape, after):
    levels, rows, cols, width = fine_shape
    return run_kernel(
        last_body,
        "last",
        [WHOLE] * 2 + [LEFT_OUT] * 2 + [WHOLE] * 3 + [LEFT_OUT] * len(after),
        [shaped(fine_shape, F32)],
        [
            pltpu.VMEM(cat.shape, F32),
            pltpu.VMEM((levels, rows, width // LANES, cols, LANES), F32),
            pltpu.VMEM((2, *own.shape[1:]), BF16),
            pltpu.SemaphoreType.DMA((2,)),
        ],
        2 * cat.shape[0] * merge_weight.shape[0] * merge_weight.shape[1],
        10_000_000,
        coarse, cot, own, there, far, cat, merge_weight, *after,
        vmem=30 * MIB,
    )[0]


def with_rows(cells, width):
    count = lax.axis_size("lat")
    above = lax.ppermute(
        cells[:, -width:], "lat", [(i, (i + 1) % count) for i in range(count)]
    )
    below = lax.ppermute(cells[:, :width], "lat", [((i + 1) % count, i) for i in range(count)])
    return above, below


def on_device(
    fine_field, head_scale, qkv_weight, out_weight, merge_weight, up_weight, down_weight, cotangent
):
    levels, lat_rows, lon_cols, channels = fine_field.shape
    coarse_width = merge_weight.shape[1]
    half_lat, half_lon = WH // 2, WW // 2
    lon_count = lax.axis_size("lon")
    me = lax.axis_index("lon")
    place = jnp.stack([(me // STRIDES[d]) % DIMS[d] for d in range(3)]).astype(jnp.int32)

    weights = jnp.stack([up_weight, down_weight.T])[:, None]
    weights = jnp.concatenate([weights, lon_swap(weights, 0, 1)], 1)
    top, bot = with_rows(fine_field, half_lat)
    tall = [
        jnp.concatenate([top[:, :, cut], fine_field[:, :, cut], bot[:, :, cut]], 1)
        for cut in (slice(lon_cols - half_lon, lon_cols), slice(0, half_lon))
    ]
    left = lax.ppermute(tall[0], "lon", [(i, (i + 1) % lon_count) for i in range(lon_count)])
    right = lax.ppermute(tall[1], "lon", [((i + 1) % lon_count, i) for i in range(lon_count)])
    up_near = gather_near(gather_mid(weights[0], 2), 1)
    down_near = gather_near(gather_mid(weights[1], 1), 2)
    cot = cotangent.reshape(-1, coarse_width)
    held, _, _ = lax.optimization_barrier((cot, left, right))
    cot_c, cot_y = lat_swap(held, 1), lat_swap(held, 2)
    skip_field, cat, coarse, normed = front(
        fine_field, top, bot, left, right, head_scale, qkv_weight, out_weight, merge_weight,
        (*up_near, *down_near, cot_c),
    )
    up_far, down_far = gather_far(up_near, 1), gather_far(down_near, 2)
    normed, up_far, down_far, cot_y = lax.optimization_barrier((normed, up_far, down_far, cot_y))
    cots = [cot, cot_c, cot_y, lat_swap(cot_y, 1)]
    normed_c, normed_y = lat_swap(normed, 1), lat_swap(normed, 2)
    up, up_t, down, near_grad, away_grad = prep(
        place, (*up_near, *up_far), (*down_near, *down_far), cots
    )
    near_hid, near_pre = feed_near(normed, normed_c, near_grad, up)
    normed_y, near_hid = lax.optimization_barrier((normed_y, near_hid))
    tokens = [normed, normed_c, normed_y, lat_swap(normed_y, 1)]

    def scatter_one(parts, digit):
        return lon_swap(parts[1], digit, 1), lon_swap(parts[3], digit, 3)

    def scatter_two(parts, came, digit):
        keep = [add_parts(parts[2 * h][0], came[h][0]) for h in range(2)]
        send = [add_parts(parts[2 * h][1], came[h][1]) for h in range(2)]
        return keep, send, (lon_swap(send[0], digit, 3), lon_swap(send[1], digit, 1))

    term_up, term_down, (near, away, send) = feed(
        place, tokens, cots, away_grad, near_hid, near_pre, up, up_t, down
    )
    there = lat_swap(send, 1)
    up_came, down_came = scatter_one(term_up, 1), scatter_one(term_down, 2)
    back_pass = add_parts(away[0], there[2])
    back_far = lat_swap(back_pass, 2)
    up_came, down_came, back_pass = lax.optimization_barrier((up_came, down_came, back_pass))
    up_keep, _, up_came = scatter_two(term_up, up_came, 1)
    down_keep, _, down_came = scatter_two(term_down, down_came, 2)
    up_halves = [add_parts(up_keep[h], up_came[h]) for h in range(2)]
    down_halves = [add_parts(down_keep[h], down_came[h]) for h in range(2)]
    up_came, down_came = lon_swap(up_halves[1], 2, 1), lon_swap(down_halves[1], 1, 1)
    out_pass = add_parts(away[1], there[3])
    out_far = lat_swap(out_pass, 2)
    held, up_halves, down_halves = lax.optimization_barrier((coarse, up_halves, down_halves))
    skip_grad = last(held, cot, near, there, back_far, cat, merge_weight, fine_field.shape, ())
    up_came, down_came, skip_grad = lax.optimization_barrier((up_came, down_came, skip_grad))
    up_pair, down_pair = add_parts(up_halves[0], up_came), add_parts(down_halves[0], down_came)
    up_end = add_parts(up_pair[0], lon_swap(up_pair[1], 2, 3))
    down_end = add_parts(down_pair[0], lon_swap(down_pair[1], 1, 3))
    both = jnp.stack([up_end, down_end], 1)
    both = both[0].astype(F32) + lon_swap(both[1], 0, 1).astype(F32)
    coarse_out = (
        coarse.astype(F32)
        + (near[1].astype(F32) + there[1].astype(F32) + out_far.astype(F32))
    ).astype(BF16)
    return (
        skip_field,
        coarse_out.reshape(levels, lat_rows // 2, lon_cols // 2, coarse_width),
        both[0],
        both[1].T,
        skip_grad,
    )


def solution(mesh):
    placed = (
        P(None, "lat", "lon", None),
        P(),
        P(),
        P(),
        P(),
        P("lon", "lat"),
        P("lat", "lon"),
        P(None, "lat", "lon", None),
    )
    return jax.shard_map(
        on_device,
        mesh=mesh,
        in_specs=placed,
        out_specs=(
            P(None, "lat", "lon", None),
            P(None, "lat", "lon", None),
            P("lon", "lat"),
            P("lat", "lon"),
            P(None, "lat", "lon", None),
        ),
        check_vma=False,
    )
```
